768 devices in a mesh: dp: 32 (over y, x), tensor: 24 (over z, core).
Axes of the slice: x: 4, y: 8, z: 12, core: 2. Of those that a mesh axis runs over, the one named last changes fastest.
Arguments:
- rollout: bfloat16 [8192, 6144], P('dp', 'tensor'), may hold values from -100 to 100
- lengths: int32 [32, 32], replicated, may hold values from 1 to 8, as said below
- packing: int32 [1024], replicated, may hold values from 0 to 1023, as said below
- norm_gain: float32 [6144], replicated, may hold values from 0.5 to 4
- query_weight: bfloat16 [6144, 6144], P(None, 'tensor'), may hold values from -0.078125 to 0.078125
- keyval_weight: bfloat16 [6144, 1536], P(None, 'tensor'), may hold values from -0.078125 to 0.078125
- out_weight: bfloat16 [6144, 6144], P('tensor'), may hold values from -0.078125 to 0.078125
Outputs:
- layer_out: bfloat16 [8192, 6144], P('dp', 'tensor')
The draws below stay inside these ranges and needn't reach their ends.
Inputs may be any that keep to these rules, and one draw needn't show every extreme that they name: lengths[s, k] is the number of tokens of response k of source s; some response has 8 tokens in every draw. `packing`: a permutation of 0 .. 1023; response r comes from source r // 32; every owner receives exactly 32 responses, exactly 1 of them from each source.
All inputs are finite; a program needn't handle non-finite values.
Results may differ from the reference program's by a relative error of at most 0.015.
Values may be sent and summed in bfloat16 or wider, within the bound.
No kernel may reach another device: no remote copies, remote signals or barrier semaphores. Data moves between devices by JAX's collectives and lax.ppermute only.
A program may use at most 64 MiB of HBM per device.

```python
import math
import jax
import jax.numpy as jnp
from jax import lax

D = 6144
HD = 128
HQ_DEV = 2
GROUP = 8
MAXLEN = 8
RPS = 32
HEADS = 48
KV_HEADS = 6
L = 256
N_DP = 32
N_TENSOR = 24


def draw_lengths(key, part):
    drawn = jax.random.randint(jax.random.fold_in(key, 11), (N_DP * RPS,), 1, MAXLEN + 1)
    longest = jax.random.randint(jax.random.fold_in(key, 12), (), 0, N_DP * RPS)
    flattened = jnp.where(jnp.arange(N_DP * RPS) == longest, MAXLEN, drawn)
    return flattened.reshape(N_DP, RPS).astype(jnp.int32)


def draw_packing(key, part):
    response_count = N_DP * RPS
    owner_order = jax.random.permutation(jax.random.fold_in(key, 21), N_DP)
    source = jnp.arange(response_count) // RPS
    within = jnp.arange(response_count) % RPS
    target = owner_order[(source + within) % N_DP]
    tiebreak = jax.random.permutation(jax.random.fold_in(key, 22), response_count)
    sort_key = target * response_count + tiebreak
    return jnp.argsort(sort_key).astype(jnp.int32)


def draw_rollout(key, part):
    noise = jax.random.normal(jax.random.fold_in(key, 31), (N_DP * L, D), jnp.float32)
    return jnp.clip(noise, -100.0, 100.0).astype(jnp.bfloat16)


def draw_norm_gain(key, part):
    drawn = 1.0 + 0.1 * jax.random.normal(jax.random.fold_in(key, 42), (D,), jnp.float32)
    return jnp.clip(drawn, 0.5, 4.0).astype(jnp.float32)


def shard_levels(rng, shape, cuts, least, high):
    gain, own = 1.0, jax.random.fold_in(rng, 6)
    for axis_at, blocks in cuts:
        steps = jnp.exp(jax.random.uniform(jax.random.fold_in(own, axis_at), (blocks,), jnp.float32, least / len(cuts), high / len(cuts)))
        gain = gain * jnp.repeat(steps, shape[axis_at] // blocks).reshape([-1 if axis == axis_at else 1 for axis in range(len(shape))])
    return gain


def centred(own_key, shape, scale, most, shards=(), kind=jnp.bfloat16):
    gain = shard_levels(own_key, shape, shards, -0.22, 0.18) if shards else 1.0
    array = jax.random.normal(own_key, shape, jnp.float32) * scale * gain
    return jnp.minimum(jnp.maximum(array, -most), most).astype(kind)


def setup_inputs(seed: int = 0) -> dict:
    key_of = jax.random.split(jax.random.key(seed), 8)
    rollout = draw_rollout(jax.random.fold_in(key_of[7], 71), 0)
    lengths = draw_lengths(jax.random.fold_in(key_of[7], 71), 0)
    packing = draw_packing(jax.random.fold_in(key_of[7], 71), 0)
    norm_gain = draw_norm_gain(jax.random.fold_in(key_of[7], 71), 0)
    query_weight = centred(key_of[4], (D, HEADS * HD), D ** -0.5, 0.078125, ((1, 24),))
    keyval_weight = centred(key_of[5], (D, 2 * KV_HEADS * HD), D ** -0.5, 0.078125, ((1, 24),))
    out_weight = centred(key_of[6], (HEADS * HD, D), (HEADS * HD) ** -0.5, 0.078125, ((0, 24),))
    return {"rollout": rollout, "lengths": lengths, "packing": packing, "norm_gain": norm_gain, "query_weight": query_weight, "keyval_weight": keyval_weight, "out_weight": out_weight}


epsilon = 1e-05
rope_base = 500000.0

def owner_map(lengths, packing, owner_id, pack_len):
    per_source = lengths.shape[1]
    chosen = lax.dynamic_slice_in_dim(packing, owner_id * per_source, per_source)
    ordered = jnp.take(lengths.reshape(-1), chosen)
    doc_start = jnp.cumsum(ordered) - ordered
    places = jnp.arange(pack_len, dtype=jnp.int32)
    inside = (places[:, None] >= doc_start[None, :]) & (places[:, None] < (doc_start + ordered)[None, :])
    is_valid = jnp.any(inside, axis=1)
    slot_of = lax.optimization_barrier(jnp.sum(jnp.where(inside, jnp.arange(per_source, dtype=jnp.int32)[None, :], 0), axis=1)).astype(jnp.int32)
    response = jnp.take(chosen, slot_of)
    position = jnp.where(is_valid, places - jnp.take(doc_start, slot_of), 0).astype(jnp.int32)
    doc_id = jnp.where(is_valid, slot_of, per_source).astype(jnp.int32)
    return (response, position, doc_id, is_valid)

def rotate(values, position, head_dim):
    half_dim = head_dim // 2
    frequency = rope_base ** (-jnp.arange(half_dim, dtype=jnp.float32) * 2.0 / head_dim)
    angles = position.astype(jnp.float32)[:, None] * frequency[None, :]
    cosine = jnp.concatenate([jnp.cos(angles), jnp.cos(angles)], axis=1)[:, None, :]
    sine_table = jnp.concatenate([jnp.sin(angles), jnp.sin(angles)], axis=1)[:, None, :]
    turned = jnp.concatenate([-values[..., half_dim:], values[..., :half_dim]], axis=-1)
    return values * cosine + turned * sine_table

def reference(rollout, lengths, packing, norm_gain, query_weight, keyval_weight, out_weight):
    per_source = lengths.shape[1]
    source_start = (jnp.cumsum(lengths, axis=1) - lengths).reshape(-1).astype(jnp.int32)
    kv_count = keyval_weight.shape[1] // (2 * HD)
    head_count = query_weight.shape[1] // HD

    def one_owner(owner_id):
        response, position, doc_id, is_valid = owner_map(lengths, packing, owner_id, L)
        global_row = response // per_source * L + jnp.take(source_start, response) + position
        packed = jnp.where(is_valid[:, None], jnp.take(rollout, global_row.astype(jnp.int32), axis=0), jnp.zeros((), jnp.bfloat16))
        widened = packed.astype(jnp.float32)
        inverse = lax.rsqrt(lax.optimization_barrier(jnp.mean(widened * widened, axis=1)) + epsilon)
        scaled = (widened * norm_gain[None, :]).astype(jnp.bfloat16)
        queries = jnp.dot(scaled, query_weight, preferred_element_type=jnp.float32) * inverse[:, None]
        keyval = (jnp.dot(scaled, keyval_weight, preferred_element_type=jnp.float32) * inverse[:, None]).astype(jnp.bfloat16)
        q_rot = rotate(queries.reshape(L, head_count, HD), position, HD).astype(jnp.bfloat16)
        k_rot = rotate(keyval[:, :kv_count * HD].astype(jnp.float32).reshape(L, kv_count, HD), position, HD).astype(jnp.bfloat16)
        value_heads = keyval[:, kv_count * HD:].reshape(L, kv_count, HD)
        shared_head = jnp.arange(head_count, dtype=jnp.int32) // GROUP
        key_full = k_rot[:, shared_head]
        value_full = value_heads[:, shared_head]
        scores = jnp.einsum('qhd,khd->hqk', q_rot.astype(jnp.float32), key_full.astype(jnp.float32)) / math.sqrt(HD)
        places = jnp.arange(L, dtype=jnp.int32)
        allowed = (doc_id[:, None] == doc_id[None, :]) & (places[None, :] <= places[:, None])
        masked = jnp.where(allowed[None], scores, -jnp.inf)
        row_max = lax.optimization_barrier(jnp.max(masked, axis=2, keepdims=True))
        exponent = jnp.exp(masked - row_max)
        weights = (exponent / lax.optimization_barrier(jnp.sum(exponent, axis=2, keepdims=True))).astype(jnp.bfloat16)
        context = jnp.einsum('hqk,khd->qhd', weights.astype(jnp.float32), value_full.astype(jnp.float32))
        context = context.astype(jnp.bfloat16).reshape(L, head_count * HD)
        groups = context.reshape(L, N_TENSOR, HQ_DEV * HD).transpose(1, 0, 2)
        out_groups = out_weight.reshape(N_TENSOR, HQ_DEV * HD, D)

        def add_group(summed, operands):
            portion = jnp.dot(operands[0], operands[1], preferred_element_type=jnp.float32).astype(jnp.bfloat16)
            portion = lax.optimization_barrier(portion)
            return (summed + portion.astype(jnp.float32), None)
        summed, unused = lax.scan(add_group, jnp.zeros((L, D), jnp.float32), (groups, out_groups))
        return jnp.where(is_valid[:, None], summed + widened, 0.0).astype(jnp.bfloat16)
    outputs = lax.map(one_owner, jnp.arange(N_DP, dtype=jnp.int32))
    return outputs.reshape(N_DP * L, D)
```

```python
import functools
import math

import jax
import jax.numpy as jnp
from jax import lax
from jax.experimental import pallas as pl
from jax.experimental.pallas import tpu as pltpu
from jax.sharding import PartitionSpec as P

D = 6144
HD = 128
MAXLEN = 8
NZ = 12
NT = 24
FS = 256
RPS = 32
KVS = 64
EPS = 1e-05
ROPE_BASE = 500000.0
AG_ROWS = 168
VMEM = 40 * 1024 * 1024

Z_GROUPS = [[z * 2 + c for z in range(NZ)] for c in range(2)]
SWAP = [(t, t ^ 1) for t in range(NT)]


def kv_round(i):
    pairs = []
    for t in range(NT):
        j = t % 2 + 2 * (t >= NT // 2)
        g = (t % (NT // 2)) // 2
        pairs.append((t, 4 * g + (i + j) % 4))
    return pairs


def swap(v):
    return lax.ppermute(v, "tensor", SWAP)


def qkv_kernel(core, mine, theirs, gain_a, gain_b, wq_a, wq_b, wk_a, wk_b, q_out, kv_out, q_acc, kv_acc, sq_acc):
    step = pl.program_id(0)

    @pl.when(step == 0)
    def _():
        q_acc[...] = jnp.zeros_like(q_acc)
        kv_acc[...] = jnp.zeros_like(kv_acc)
        sq_acc[...] = jnp.zeros_like(sq_acc)

    for x_ref, gain, wq, wk in ((mine, gain_a, wq_a, wk_a), (theirs, gain_b, wq_b, wk_b)):
        x = x_ref[0].astype(jnp.float32)
        square = x * x
        sq_acc[...] += square[:, :128] + square[:, 128:]
        scaled = (x * gain[0]).astype(jnp.bfloat16)
        q_acc[...] += jnp.dot(scaled, wq[...], preferred_element_type=jnp.float32)
        kv_acc[...] += lax.dot_general(
            scaled, wk[...], (((1,), (1,)), ((), ())), preferred_element_type=jnp.float32
        )

    @pl.when(step == NZ - 1)
    def _():
        inverse = lax.rsqrt(jnp.sum(sq_acc[...], axis=1, keepdims=True) / D + EPS)
        q_out[...] = q_acc[...] * inverse
        kv_out[...] = (kv_acc[...] * inverse).astype(jnp.bfloat16)


def project(core, mine, theirs, gain, wq, wk_t):
    rows = mine.shape[1]
    own = lambda i, c: (2 * i + c[0], 0)
    sib = lambda i, c: (2 * i + 1 - c[0], 0)
    own3 = lambda i, c: (2 * i + c[0], 0, 0)
    sib3 = lambda i, c: (2 * i + 1 - c[0], 0, 0)
    own_t = lambda i, c: (0, 2 * i + c[0])
    sib_t = lambda i, c: (0, 2 * i + 1 - c[0])
    block = lambda i, c: (i, 0, 0)
    whole = lambda i, c: (0, 0)
    gain3 = gain.reshape(NT, 1, FS)
    return pl.pallas_call(
        qkv_kernel,
        grid_spec=pltpu.PrefetchScalarGridSpec(
            num_scalar_prefetch=1,
            grid=(NZ,),
            in_specs=[
                pl.BlockSpec((1, rows, FS), block),
                pl.BlockSpec((1, rows, FS), block),
                pl.BlockSpec((1, 1, FS), own3),
                pl.BlockSpec((1, 1, FS), sib3),
                pl.BlockSpec((FS, FS), own),
                pl.BlockSpec((FS, FS), sib),
                pl.BlockSpec((KVS, FS), own_t),
                pl.BlockSpec((KVS, FS), sib_t),
            ],
            out_specs=[pl.BlockSpec((rows, FS), whole), pl.BlockSpec((rows, KVS), whole)],
            scratch_shapes=[
                pltpu.VMEM((rows, FS), jnp.float32),
                pltpu.VMEM((rows, KVS), jnp.float32),
                pltpu.VMEM((rows, 128), jnp.float32),
            ],
        ),
        out_shape=[
            jax.ShapeDtypeStruct((rows, FS), jnp.float32),
            jax.ShapeDtypeStruct((rows, KVS), jnp.bfloat16),
        ],
        compiler_params=pltpu.CompilerParams(vmem_limit_bytes=VMEM),
        cost_estimate=pl.CostEstimate(
            flops=2 * rows * D * (FS + KVS), bytes_accessed=2 * D * (rows + FS + KVS), transcendentals=rows
        ),
        name="project",
    )(core, mine, theirs, gain3, gain3, wq, wq, wk_t, wk_t)


def attention_kernel(order, q_ref, r0, r1, r2, r3, cos_ref, sin_ref, col_ref, row_ref, out_ref):
    rows = q_ref.shape[0]
    m = order[0]
    got = [r[...].astype(jnp.float32) for r in (r0, r1, r2, r3)]

    def piece(j):
        at = lax.rem(m - j + 4, 4)
        out = got[0]
        for i in range(1, 4):
            out = jnp.where(at == i, got[i], out)
        return out

    keys = jnp.concatenate([piece(0), piece(1)], axis=1)
    values = jnp.concatenate([piece(2), piece(3)], axis=1).astype(jnp.bfloat16)
    cosine = cos_ref[...]
    sine = sin_ref[...]

    def turn(v):
        turned = jnp.concatenate([-v[:, HD // 2 :], v[:, : HD // 2]], axis=1)
        return (v * cosine + turned * sine).astype(jnp.bfloat16)

    k_rot = turn(keys)
    doc_q = col_ref[...]
    doc_k = row_ref[...]
    place_q = lax.broadcasted_iota(jnp.int32, (rows, rows), 0)
    place_k = lax.broadcasted_iota(jnp.int32, (rows, rows), 1)
    allowed = (doc_q == doc_k) & (place_k <= place_q)
    for h in range(2):
        q_rot = turn(q_ref[:, h * HD : (h + 1) * HD])
        scores = lax.dot_general(
            q_rot, k_rot, (((1,), (1,)), ((), ())), preferred_element_type=jnp.float32
        ) / math.sqrt(HD)
        masked = jnp.where(allowed, scores, -jnp.inf)
        exponent = jnp.exp(masked - jnp.max(masked, axis=1, keepdims=True))
        weights = (exponent / jnp.sum(exponent, axis=1, keepdims=True)).astype(jnp.bfloat16)
        context = jnp.dot(weights, values, preferred_element_type=jnp.float32)
        out_ref[:, h * HD : (h + 1) * HD] = context.astype(jnp.bfloat16)


def attend(order, q, pieces, cosine, sine, doc):
    rows = q.shape[0]
    vm = pl.BlockSpec(memory_space=pltpu.VMEM)
    return pl.pallas_call(
        attention_kernel,
        in_specs=[pl.BlockSpec(memory_space=pltpu.SMEM)] + [vm] * 9,
        out_specs=vm,
        out_shape=jax.ShapeDtypeStruct((rows, FS), jnp.bfloat16),
        compiler_params=pltpu.CompilerParams(vmem_limit_bytes=VMEM),
        cost_estimate=pl.CostEstimate(
            flops=8 * rows * rows * HD, bytes_accessed=4 * rows * FS, transcendentals=2 * rows * rows
        ),
        name="attend",
    )(order, q, *pieces, cosine, sine, doc[:, None], doc[None, :])


def out_kernel(core, mine, theirs, w_mine, w_theirs, out_ref):
    total = jnp.dot(mine[...], w_mine[...], preferred_element_type=jnp.float32)
    total += jnp.dot(theirs[...], w_theirs[...], preferred_element_type=jnp.float32)
    out_ref[0] = total.astype(jnp.bfloat16)


def out_project(core, mine, theirs, w_mine, w_theirs):
    rows = mine.shape[0]
    return pl.pallas_call(
        out_kernel,
        grid_spec=pltpu.PrefetchScalarGridSpec(
            num_scalar_prefetch=1,
            grid=(NZ,),
            in_specs=[
                pl.BlockSpec((rows, FS), lambda i, c: (0, 0)),
                pl.BlockSpec((rows, FS), lambda i, c: (0, 0)),
                pl.BlockSpec((FS, FS), lambda i, c: (0, 2 * i + c[0])),
                pl.BlockSpec((FS, FS), lambda i, c: (0, i)),
            ],
            out_specs=pl.BlockSpec((1, rows, FS), lambda i, c: (i, 0, 0)),
        ),
        out_shape=jax.ShapeDtypeStruct((NZ, rows, FS), jnp.bfloat16),
        compiler_params=pltpu.CompilerParams(vmem_limit_bytes=VMEM),
        cost_estimate=pl.CostEstimate(
            flops=4 * rows * FS * D // 2, bytes_accessed=2 * D * (rows + 2 * FS), transcendentals=0
        ),
        name="out_project",
    )(core, mine, theirs, w_mine, w_theirs)


def gather_rows(x):
    rows = x.shape[0]
    first = min(rows, AG_ROWS)
    rest = None
    if rows > first:
        tail = jnp.broadcast_to(x[first:][None], (NZ, rows - first, FS))
        rest = lax.all_to_all(
            tail, "tensor", split_axis=0, concat_axis=0, tiled=True, axis_index_groups=Z_GROUPS
        )
    got = lax.all_gather(x[:first], "tensor", axis=0, axis_index_groups=Z_GROUPS)
    if rest is None:
        return got
    return jnp.concatenate([got, rest], axis=1)


def layer(rows, rollout, lengths, packing, norm_gain, query_weight, keyval_weight, out_weight):
    source = lax.axis_index("dp")
    tensor_index = lax.axis_index("tensor")
    core = (tensor_index % 2).astype(jnp.int32).reshape(1)
    x = rollout[:rows]

    ow4 = out_weight.reshape(FS, NZ, 2, FS)
    send = lax.dynamic_index_in_dim(ow4, 1 - core[0], 2, keepdims=False).reshape(FS, NZ * FS)
    ow_theirs = swap(send)

    mine = gather_rows(x)
    theirs = swap(mine)
    q, keyval = project(core, mine, theirs, norm_gain, query_weight, keyval_weight.T)
    pieces = [lax.ppermute(keyval, "tensor", kv_round(i)) for i in range(4)]

    my_len = lax.dynamic_index_in_dim(lengths, source, 0, keepdims=False)
    earlier = jnp.arange(RPS)[None, :] < jnp.arange(RPS)[:, None]
    start = jnp.sum(jnp.where(earlier, my_len[None, :], 0), axis=1)
    places = jnp.arange(rows, dtype=jnp.int32)
    doc = jnp.sum((places[:, None] >= (start + my_len)[None, :]).astype(jnp.int32), axis=1)
    begun = jnp.max(jnp.where(start[None, :] <= places[:, None], start[None, :], 0), axis=1)
    position = jnp.where(doc < RPS, places - begun, 0)
    frequency = ROPE_BASE ** (-jnp.arange(HD // 2, dtype=jnp.float32) * 2.0 / HD)
    angles = position.astype(jnp.float32)[:, None] * jnp.concatenate([frequency, frequency])[None, :]
    context = attend(
        (tensor_index % 4).astype(jnp.int32).reshape(1), q, pieces, jnp.cos(angles), jnp.sin(angles), doc
    )

    partial = out_project(core, context, swap(context), out_weight, ow_theirs)
    parts = lax.all_to_all(
        partial, "tensor", split_axis=0, concat_axis=0, tiled=True, axis_index_groups=Z_GROUPS
    )
    result = (jnp.sum(parts.astype(jnp.float32), axis=0) + x.astype(jnp.float32)).astype(jnp.bfloat16)

    pack = packing.reshape(RPS, RPS)
    of_mine = pack // RPS == source
    which = jnp.sum(jnp.where(of_mine, pack % RPS, 0), axis=1)
    chosen = which[:, None] == jnp.arange(RPS)[None, :]
    o_start = jnp.sum(jnp.where(chosen, start[None, :], 0), axis=1)
    o_len = jnp.sum(jnp.where(chosen, my_len[None, :], 0), axis=1)
    slot = jnp.arange(MAXLEN, dtype=jnp.int32)
    row_of = jnp.where(slot[None, :] < o_len[:, None], o_start[:, None] + slot[None, :], -1).reshape(-1)
    pick = (row_of[:, None] == places[None, :]).astype(jnp.bfloat16)
    outgoing = jnp.dot(pick, result, preferred_element_type=jnp.float32).astype(jnp.bfloat16)
    return outgoing


def body(rollout, lengths, packing, norm_gain, query_weight, keyval_weight, out_weight):
    owner = lax.axis_index("dp")
    total = rollout.shape[0]
    outgoing = layer(
        total, rollout, lengths, packing, norm_gain, query_weight, keyval_weight, out_weight
    )
    incoming = lax.all_to_all(
        outgoing.reshape(RPS, MAXLEN, FS), "dp", split_axis=0, concat_axis=0, tiled=True
    ).reshape(RPS * MAXLEN, FS)

    chosen = lax.dynamic_index_in_dim(packing.reshape(RPS, RPS), owner, 0, keepdims=False)
    from_source = chosen // RPS
    is_source = from_source[:, None] == jnp.arange(RPS)[None, :]
    of_source = jnp.sum(jnp.where(is_source[:, :, None], lengths[None], 0), axis=1)
    is_k = (chosen % RPS)[:, None] == jnp.arange(RPS)[None, :]
    length = jnp.sum(jnp.where(is_k, of_source, 0), axis=1)
    earlier = jnp.arange(RPS)[None, :] < jnp.arange(RPS)[:, None]
    start = jnp.sum(jnp.where(earlier, length[None, :], 0), axis=1)
    places = jnp.arange(total, dtype=jnp.int32)
    inside = (places[:, None] >= start[None, :]) & (places[:, None] < (start + length)[None, :])
    valid = jnp.any(inside, axis=1)
    at = jnp.sum(jnp.where(inside, from_source[None, :] * MAXLEN + places[:, None] - start[None, :], 0), axis=1)
    at = jnp.where(valid, at, -1)
    pick = (at[:, None] == jnp.arange(RPS * MAXLEN)[None, :]).astype(jnp.bfloat16)
    return jnp.dot(pick, incoming, preferred_element_type=jnp.float32).astype(jnp.bfloat16)


def solution(mesh):
    in_specs = (
        P("dp", "tensor"),
        P(),
        P(),
        P(),
        P(None, "tensor"),
        P(None, "tensor"),
        P("tensor", None),
    )
    out_specs = P("dp", "tensor")
    return jax.shard_map(body, mesh=mesh, in_specs=in_specs, out_specs=out_specs, check_vma=False)
```

```python
import functools
import math

import jax
import jax.numpy as jnp
from jax import lax
from jax.experimental import pallas as pl
from jax.experimental.pallas import tpu as pltpu
from jax.sharding import PartitionSpec as P

D = 6144
HD = 128
MAXLEN = 8
NZ = 12
NT = 24
FS = 256
RPS = 32
KVS = 64
EPS = 1e-05
ROPE_BASE = 500000.0
AG_ROWS = 168
VMEM = 40 * 1024 * 1024

Z_GROUPS = [[z * 2 + c for z in range(NZ)] for c in range(2)]
SWAP = [(t, t ^ 1) for t in range(NT)]


STEPS = 3
PER = NZ // STEPS
CAPS = (168, 176, 192, 256)


def kv_pairs(first):
    pairs = []
    for z in range(NZ):
        g, value = z % (NZ // 2), z // (NZ // 2)
        to = 2 * g + (value if first else 1 - value)
        pairs += [(2 * z + c, 2 * to + c) for c in range(2)]
    return pairs


def swap(v):
    return lax.ppermute(v, "tensor", SWAP)


def rows_of(refs, j, side):
    head, tail = refs
    x = head[j].astype(jnp.float32)
    if tail is not None:
        x = jnp.concatenate([x, tail[2 * j + side].astype(jnp.float32)], axis=0)
    return x


def kv_kernel(has_tail, core, mine, theirs, *rest):
    if has_tail:
        tail, *rest = rest
    else:
        tail = None
    gain, wk_m, wk_t, kv_out, inv_out, kv_acc, sq_acc = rest
    step = pl.program_id(0)
    c = core[0]

    @pl.when(step == 0)
    def _():
        kv_acc[...] = jnp.zeros_like(kv_acc)
        sq_acc[...] = jnp.zeros_like(sq_acc)

    total, squares = kv_acc[...], sq_acc[...]
    for j in range(PER):
        for x_ref, side in ((mine, c), (theirs, 1 - c)):
            x = rows_of((x_ref, tail), j, side)
            square = x * x
            squares += square[:, :128] + square[:, 128:]
            scaled = (x * gain[2 * j + side]).astype(jnp.bfloat16)
            at = pl.ds(pl.multiple_of((2 * j + side) * FS, FS), FS)
            w = jnp.concatenate([wk_m[:, at], wk_t[:, at]], axis=0)
            total += lax.dot_general(
                scaled, w, (((1,), (1,)), ((), ())), preferred_element_type=jnp.float32
            )
    kv_acc[...] = total
    sq_acc[...] = squares

    @pl.when(step == STEPS - 1)
    def _():
        inverse = lax.rsqrt(jnp.sum(squares, axis=1, keepdims=True) / D + EPS)
        out = total * inverse
        turned = jnp.concatenate([out[:, KVS:], out[:, :KVS]], axis=1)
        kv_out[...] = jnp.where(c == 0, out, turned).astype(jnp.bfloat16)
        inv_out[...] = jnp.broadcast_to(inverse, inv_out.shape)


def q_kernel(has_tail, core, mine, theirs, *rest):
    if has_tail:
        tail, *rest = rest
    else:
        tail = None
    gain, wq_m, wq_t, inv, q_out, q_acc = rest
    step = pl.program_id(0)
    c = core[0]

    @pl.when(step == 0)
    def _():
        q_acc[...] = jnp.zeros_like(q_acc)

    total = q_acc[...]
    for j in range(PER):
        for x_ref, wq, side in ((mine, wq_m, c), (theirs, wq_t, 1 - c)):
            x = rows_of((x_ref, tail), j, side)
            scaled = (x * gain[2 * j + side]).astype(jnp.bfloat16)
            total += jnp.dot(scaled, wq[j, 0], preferred_element_type=jnp.float32)
    q_acc[...] = total

    @pl.when(step == STEPS - 1)
    def _():
        for h in range(2):
            q_out[:, h * HD : (h + 1) * HD] = total[:, h * HD : (h + 1) * HD] * inv[...]


def x_specs(mine, tail):
    specs = [pl.BlockSpec((PER, mine.shape[1], FS), lambda i, c: (i, 0, 0))] * 2
    if tail is not None:
        specs.append(pl.BlockSpec((2 * PER, tail.shape[1], FS), lambda i, c: (i, 0, 0)))
    specs.append(pl.BlockSpec((2 * PER, 1, FS), lambda i, c: (i, 0, 0)))
    return specs


def project_kv(core, mine, theirs, tail, gain, wk_m, wk_t):
    rows = mine.shape[1] + (0 if tail is None else tail.shape[1])
    whole = pl.BlockSpec((rows, HD), lambda i, c: (0, 0))
    wk_spec = pl.BlockSpec((KVS, 2 * PER * FS), lambda i, c: (0, i))
    return pl.pallas_call(
        functools.partial(kv_kernel, tail is not None),
        grid_spec=pltpu.PrefetchScalarGridSpec(
            num_scalar_prefetch=1,
            grid=(STEPS,),
            in_specs=x_specs(mine, tail) + [wk_spec, wk_spec],
            out_specs=[whole, whole],
            scratch_shapes=[pltpu.VMEM((rows, HD), jnp.float32), pltpu.VMEM((rows, HD), jnp.float32)],
        ),
        out_shape=[
            jax.ShapeDtypeStruct((rows, HD), jnp.bfloat16),
            jax.ShapeDtypeStruct((rows, HD), jnp.float32),
        ],
        compiler_params=pltpu.CompilerParams(vmem_limit_bytes=VMEM),
        cost_estimate=pl.CostEstimate(
            flops=2 * rows * D * HD, bytes_accessed=2 * D * (rows + HD), transcendentals=rows
        ),
        name="project_kv",
    )(core, mine, theirs, *([] if tail is None else [tail]), gain, wk_m, wk_t)


def project_q(core, mine, theirs, tail, gain, wq, inverse):
    rows = inverse.shape[0]
    wq4 = wq.reshape(NZ, 2, FS, FS)
    return pl.pallas_call(
        functools.partial(q_kernel, tail is not None),
        grid_spec=pltpu.PrefetchScalarGridSpec(
            num_scalar_prefetch=1,
            grid=(STEPS,),
            in_specs=x_specs(mine, tail)
            + [
                pl.BlockSpec((PER, 1, FS, FS), lambda i, c: (i, c[0], 0, 0)),
                pl.BlockSpec((PER, 1, FS, FS), lambda i, c: (i, 1 - c[0], 0, 0)),
                pl.BlockSpec((rows, HD), lambda i, c: (0, 0)),
            ],
            out_specs=pl.BlockSpec((rows, FS), lambda i, c: (0, 0)),
            scratch_shapes=[pltpu.VMEM((rows, FS), jnp.float32)],
        ),
        out_shape=jax.ShapeDtypeStruct((rows, FS), jnp.float32),
        compiler_params=pltpu.CompilerParams(vmem_limit_bytes=VMEM),
        cost_estimate=pl.CostEstimate(
            flops=2 * rows * D * FS, bytes_accessed=2 * D * (rows + FS), transcendentals=0
        ),
        name="project_q",
    )(core, mine, theirs, *([] if tail is None else [tail]), gain, wq4, wq4, inverse)


def attention_kernel(odd, q_ref, first, second, cos_ref, sin_ref, col_ref, row_ref, out_ref):
    rows = q_ref.shape[0]
    one, two = first[...].astype(jnp.float32), second[...].astype(jnp.float32)
    swapped = odd[0] == 1
    keys = jnp.where(swapped, two, one)
    values = jnp.where(swapped, one, two).astype(jnp.bfloat16)
    cosine = cos_ref[...]
    sine = sin_ref[...]

    def turn(v):
        turned = jnp.concatenate([-v[:, HD // 2 :], v[:, : HD // 2]], axis=1)
        return (v * cosine + turned * sine).astype(jnp.bfloat16)

    k_rot = turn(keys)
    doc_q = col_ref[...]
    doc_k = row_ref[...]
    place_q = lax.broadcasted_iota(jnp.int32, (rows, rows), 0)
    place_k = lax.broadcasted_iota(jnp.int32, (rows, rows), 1)
    allowed = (doc_q == doc_k) & (place_k <= place_q)
    for h in range(2):
        q_rot = turn(q_ref[:, h * HD : (h + 1) * HD])
        scores = lax.dot_general(
            q_rot, k_rot, (((1,), (1,)), ((), ())), preferred_element_type=jnp.float32
        ) / math.sqrt(HD)
        masked = jnp.where(allowed, scores, -jnp.inf)
        exponent = jnp.exp(masked - jnp.max(masked, axis=1, keepdims=True))
        weights = (exponent / jnp.sum(exponent, axis=1, keepdims=True)).astype(jnp.bfloat16)
        context = jnp.dot(weights, values, preferred_element_type=jnp.float32)
        out_ref[:, h * HD : (h + 1) * HD] = context.astype(jnp.bfloat16)


def attend(odd, q, first, second, cosine, sine, doc):
    rows = q.shape[0]
    vm = pl.BlockSpec(memory_space=pltpu.VMEM)
    return pl.pallas_call(
        attention_kernel,
        in_specs=[pl.BlockSpec(memory_space=pltpu.SMEM)] + [vm] * 7,
        out_specs=vm,
        out_shape=jax.ShapeDtypeStruct((rows, FS), jnp.bfloat16),
        compiler_params=pltpu.CompilerParams(vmem_limit_bytes=VMEM),
        cost_estimate=pl.CostEstimate(
            flops=8 * rows * rows * HD, bytes_accessed=4 * rows * FS, transcendentals=2 * rows * rows
        ),
        name="attend",
    )(odd, q, first, second, cosine, sine, doc[:, None], doc[None, :])


def out_kernel(core, mine, theirs, *rest):
    w_mine, w_theirs, out_ref = rest[:PER], rest[PER : 2 * PER], rest[-1]
    for j in range(PER):
        total = jnp.dot(mine[...], w_mine[j][...], preferred_element_type=jnp.float32)
        total += jnp.dot(theirs[...], w_theirs[j][...], preferred_element_type=jnp.float32)
        out_ref[j] = total.astype(jnp.bfloat16)


def out_project(core, mine, theirs, w_mine, w_theirs):
    rows = mine.shape[0]
    context = pl.BlockSpec((rows, FS), lambda i, c: (0, 0))
    weights = [
        pl.BlockSpec((FS, FS), lambda i, c, j=j: (0, 2 * (PER * i + j) + c[0])) for j in range(PER)
    ]
    return pl.pallas_call(
        out_kernel,
        grid_spec=pltpu.PrefetchScalarGridSpec(
            num_scalar_prefetch=1,
            grid=(STEPS,),
            in_specs=[context, context] + weights + weights,
            out_specs=pl.BlockSpec((PER, rows, FS), lambda i, c: (i, 0, 0)),
        ),
        out_shape=jax.ShapeDtypeStruct((NZ, rows, FS), jnp.bfloat16),
        compiler_params=pltpu.CompilerParams(vmem_limit_bytes=VMEM),
        cost_estimate=pl.CostEstimate(
            flops=2 * rows * FS * D, bytes_accessed=D * (rows + 2 * FS), transcendentals=0
        ),
        name="out_project",
    )(core, mine, theirs, *[w_mine] * PER, *[w_theirs] * PER)


def gather_rows(x):
    rows = x.shape[0]
    tail = None
    if rows > AG_ROWS:
        last = jnp.broadcast_to(x[AG_ROWS:][None], (NT, rows - AG_ROWS, FS))
        tail = lax.all_to_all(last, "tensor", split_axis=0, concat_axis=0, tiled=True)
    return lax.all_gather(x[:AG_ROWS], "tensor", axis=0, axis_index_groups=Z_GROUPS), tail


def layer(rows, rollout, lengths, packing, norm_gain, query_weight, keyval_weight, out_weight):
    source = lax.axis_index("dp")
    tensor_index = lax.axis_index("tensor")
    core = (tensor_index % 2).astype(jnp.int32).reshape(1)
    x = rollout[:rows]

    mine, tail = gather_rows(x)
    theirs = swap(mine)
    gain = norm_gain.reshape(NT, 1, FS)
    wk = keyval_weight.T
    keyval, inverse = project_kv(core, mine, theirs, tail, gain, wk, swap(wk))
    first = lax.ppermute(keyval, "tensor", kv_pairs(True))
    second = lax.ppermute(keyval, "tensor", kv_pairs(False))
    q = project_q(core, mine, theirs, tail, gain, query_weight, inverse)

    my_len = lax.dynamic_index_in_dim(lengths, source, 0, keepdims=False)
    earlier = jnp.arange(RPS)[None, :] < jnp.arange(RPS)[:, None]
    start = jnp.sum(jnp.where(earlier, my_len[None, :], 0), axis=1)
    places = jnp.arange(rows, dtype=jnp.int32)
    doc = jnp.sum((places[:, None] >= (start + my_len)[None, :]).astype(jnp.int32), axis=1)
    begun = jnp.max(jnp.where(start[None, :] <= places[:, None], start[None, :], 0), axis=1)
    position = jnp.where(doc < RPS, places - begun, 0)
    frequency = ROPE_BASE ** (-jnp.arange(HD // 2, dtype=jnp.float32) * 2.0 / HD)
    angles = position.astype(jnp.float32)[:, None] * jnp.concatenate([frequency, frequency])[None, :]
    odd = (tensor_index // 2 % 2).astype(jnp.int32).reshape(1)
    context = attend(odd, q, first, second, jnp.cos(angles), jnp.sin(angles), doc)
    partial = out_project(core, context, swap(context), out_weight, swap(out_weight))
    parts = lax.all_to_all(
        partial, "tensor", split_axis=0, concat_axis=0, tiled=True, axis_index_groups=Z_GROUPS
    )
    result = (jnp.sum(parts.astype(jnp.float32), axis=0) + x.astype(jnp.float32)).astype(jnp.bfloat16)

    pack = packing.reshape(RPS, RPS)
    of_mine = pack // RPS == source
    which = jnp.sum(jnp.where(of_mine, pack % RPS, 0), axis=1)
    chosen = which[:, None] == jnp.arange(RPS)[None, :]
    o_start = jnp.sum(jnp.where(chosen, start[None, :], 0), axis=1)
    o_len = jnp.sum(jnp.where(chosen, my_len[None, :], 0), axis=1)
    slot = jnp.arange(MAXLEN, dtype=jnp.int32)
    row_of = jnp.where(slot[None, :] < o_len[:, None], o_start[:, None] + slot[None, :], -1).reshape(-1)
    pick = (row_of[:, None] == places[None, :]).astype(jnp.bfloat16)
    outgoing = jnp.dot(pick, result, preferred_element_type=jnp.float32).astype(jnp.bfloat16)
    return outgoing


def body(rollout, lengths, packing, norm_gain, query_weight, keyval_weight, out_weight):
    owner = lax.axis_index("dp")
    total = rollout.shape[0]
    longest = jnp.max(jnp.sum(lengths, axis=1))
    size = sum((longest > cap).astype(jnp.int32) for cap in CAPS[:-1])
    outgoing = lax.switch(
        size,
        [functools.partial(layer, cap) for cap in CAPS],
        rollout, lengths, packing, norm_gain, query_weight, keyval_weight, out_weight,
    )
    incoming = lax.all_to_all(
        outgoing.reshape(RPS, MAXLEN, FS), "dp", split_axis=0, concat_axis=0, tiled=True
    ).reshape(RPS * MAXLEN, FS)

    chosen = lax.dynamic_index_in_dim(packing.reshape(RPS, RPS), owner, 0, keepdims=False)
    from_source = chosen // RPS
    is_source = from_source[:, None] == jnp.arange(RPS)[None, :]
    of_source = jnp.sum(jnp.where(is_source[:, :, None], lengths[None], 0), axis=1)
    is_k = (chosen % RPS)[:, None] == jnp.arange(RPS)[None, :]
    length = jnp.sum(jnp.where(is_k, of_source, 0), axis=1)
    earlier = jnp.arange(RPS)[None, :] < jnp.arange(RPS)[:, None]
    start = jnp.sum(jnp.where(earlier, length[None, :], 0), axis=1)
    places = jnp.arange(total, dtype=jnp.int32)
    inside = (places[:, None] >= start[None, :]) & (places[:, None] < (start + length)[None, :])
    valid = jnp.any(inside, axis=1)
    at = jnp.sum(jnp.where(inside, from_source[None, :] * MAXLEN + places[:, None] - start[None, :], 0), axis=1)
    at = jnp.where(valid, at, -1)
    pick = (at[:, None] == jnp.arange(RPS * MAXLEN)[None, :]).astype(jnp.bfloat16)
    return jnp.dot(pick, incoming, preferred_element_type=jnp.float32).astype(jnp.bfloat16)


def solution(mesh):
    in_specs = (
        P("dp", "tensor"),
        P(),
        P(),
        P(),
        P(None, "tensor"),
        P(None, "tensor"),
        P("tensor", None),
    )
    out_specs = P("dp", "tensor")
    return jax.shard_map(body, mesh=mesh, in_specs=in_specs, out_specs=out_specs, check_vma=False)
```

```python
import functools
import math

import jax
import jax.numpy as jnp
import numpy as np
from jax import lax
from jax.experimental import pallas as pl
from jax.experimental.pallas import tpu as pltpu
from jax.sharding import PartitionSpec as P

D = 6144
HD = 128
MAXLEN = 8
NZ = 12
NT = 24
FS = 256
RPS = 32
KVS = 64
EPS = 1e-05
ROPE_BASE = 500000.0
AG_ROWS = 168
VMEM = 56 * 1024 * 1024

Z_GROUPS = [[z * 2 + c for z in range(NZ)] for c in range(2)]
FAR = 4
FAR_GROUPS = [[(3 * k + r) * 2 + c for k in range(FAR)] for r in range(3) for c in range(2)]
SWAP = [(t, t ^ 1) for t in range(NT)]


STEPS = 3
PER = NZ // STEPS
CAPS = (168, 176, 192, 256)


def rope_tables():
    frequency = ROPE_BASE ** (-np.arange(HD // 2) * 2.0 / HD)
    angles = np.arange(MAXLEN)[:, None] * np.concatenate([frequency, frequency])[None, :]
    sign = np.where(np.arange(HD) < HD // 2, -1.0, 1.0)[None, :]
    return np.cos(angles).astype(np.float32), (np.sin(angles) * sign).astype(np.float32)


def turn(v, cosine, sine):
    turned = jnp.concatenate([v[:, HD // 2 :], v[:, : HD // 2]], axis=1)
    return (v * cosine + turned * sine).astype(jnp.bfloat16)


def documents(lengths, source, rows):
    own = lengths[pl.ds(source, 1), :].astype(jnp.float32)
    first = lax.broadcasted_iota(jnp.int32, (RPS, RPS), 0)
    second = lax.broadcasted_iota(jnp.int32, (RPS, RPS), 1)
    column = jnp.sum(jnp.where(first == second, own, 0.0), axis=1, keepdims=True)
    end = jnp.sum(jnp.where(first <= second, column, 0.0), axis=0, keepdims=True)
    end_column = jnp.sum(jnp.where(second <= first, own, 0.0), axis=1, keepdims=True)
    start = end - own
    place = lax.broadcasted_iota(jnp.int32, (rows, RPS), 0).astype(jnp.float32)
    doc = jnp.sum(jnp.where(place >= end, 1.0, 0.0), axis=1, keepdims=True)
    begun = jnp.max(jnp.where(start <= place, start, 0.0), axis=1, keepdims=True)
    position = jnp.where(doc < RPS, place[:, :1] - begun, 0.0)
    along = lax.broadcasted_iota(jnp.int32, (RPS, rows), 1).astype(jnp.float32)
    doc_row = jnp.sum(jnp.where(along >= end_column, 1.0, 0.0), axis=0, keepdims=True)
    return doc, position, doc_row


def kv_pairs(first):
    pairs = []
    for z in range(NZ):
        g, value = z % (NZ // 2), z // (NZ // 2)
        to = 2 * g + (value if first else 1 - value)
        pairs += [(2 * z + c, 2 * to + c) for c in range(2)]
    return pairs


def swap(v):
    return lax.ppermute(v, "tensor", SWAP)


def rows_of(refs, j, side):
    head, tail = refs
    x = head[j].astype(jnp.float32)
    if tail is not None:
        x = jnp.concatenate([x, tail[2 * j + side].astype(jnp.float32)], axis=0)
    return x


def kv_kernel(has_tail, core, mine, theirs, *rest):
    if has_tail:
        tail, *rest = rest
    else:
        tail = None
    gain, wk_m, wk_t, kv_out, inv_out, kv_acc, sq_acc = rest
    step = pl.program_id(0)
    c = core[0]

    @pl.when(step == 0)
    def _():
        kv_acc[...] = jnp.zeros_like(kv_acc)
        sq_acc[...] = jnp.zeros_like(sq_acc)

    total, squares = kv_acc[...], sq_acc[...]
    for j in range(PER):
        for x_ref, side in ((mine, c), (theirs, 1 - c)):
            x = rows_of((x_ref, tail), j, side)
            square = x * x
            squares += square[:, :128] + square[:, 128:]
            scaled = (x * gain[2 * j + side]).astype(jnp.bfloat16)
            at = pl.ds(pl.multiple_of((2 * j + side) * FS, FS), FS)
            w = jnp.concatenate([wk_m[:, at], wk_t[:, at]], axis=0)
            total += lax.dot_general(
                scaled, w, (((1,), (1,)), ((), ())), preferred_element_type=jnp.float32
            )
    kv_acc[...] = total
    sq_acc[...] = squares

    @pl.when(step == STEPS - 1)
    def _():
        inverse = lax.rsqrt(jnp.sum(squares, axis=1, keepdims=True) / D + EPS)
        out = total * inverse
        turned = jnp.concatenate([out[:, KVS:], out[:, :KVS]], axis=1)
        kv_out[...] = jnp.where(c == 0, out, turned).astype(jnp.bfloat16)
        inv_out[...] = jnp.broadcast_to(inverse, inv_out.shape)


def q_kernel(has_tail, core, mine, theirs, *rest):
    if has_tail:
        tail, *rest = rest
    else:
        tail = None
    gain, wq_m, wq_t, inv, lengths, cos_t, sin_t, q_out, cos_out, sin_out, bias_out, q_acc = rest
    step = pl.program_id(0)
    c = core[0]
    rows = q_acc.shape[0]

    @pl.when(step == 0)
    def _():
        q_acc[...] = jnp.zeros_like(q_acc)
        doc, position, doc_row = documents(lengths, core[3], rows)
        cosine = jnp.broadcast_to(cos_t[0:1], (rows, HD))
        sine = jnp.broadcast_to(sin_t[0:1], (rows, HD))
        for m in range(1, MAXLEN):
            here = jnp.broadcast_to(position == m, (rows, HD))
            cosine = jnp.where(here, cos_t[m : m + 1], cosine)
            sine = jnp.where(here, sin_t[m : m + 1], sine)
        cos_out[...] = cosine
        sin_out[...] = sine
        place_q = lax.broadcasted_iota(jnp.int32, (rows, rows), 0)
        place_k = lax.broadcasted_iota(jnp.int32, (rows, rows), 1)
        allowed = (doc == doc_row) & (place_k <= place_q)
        bias_out[...] = jnp.where(allowed, 0.0, -jnp.inf)

    total = q_acc[...]
    for j in range(PER):
        for x_ref, wq, side in ((mine, wq_m, c), (theirs, wq_t, 1 - c)):
            x = rows_of((x_ref, tail), j, side)
            scaled = (x * gain[2 * j + side]).astype(jnp.bfloat16)
            total += jnp.dot(scaled, wq[j, 0], preferred_element_type=jnp.float32)
    q_acc[...] = total

    @pl.when(step == STEPS - 1)
    def _():
        for h in range(2):
            head = total[:, h * HD : (h + 1) * HD] * inv[...]
            q_out[:, h * HD : (h + 1) * HD] = turn(head, cos_out[...], sin_out[...])


def x_specs(mine, tail):
    specs = [pl.BlockSpec((PER, mine.shape[1], FS), lambda i, c: (i, 0, 0))] * 2
    if tail is not None:
        specs.append(pl.BlockSpec((2 * PER, tail.shape[1], FS), lambda i, c: (i, 0, 0)))
    specs.append(pl.BlockSpec((2 * PER, 1, FS), lambda i, c: (i, 0, 0)))
    return specs


def project_kv(core, mine, theirs, tail, gain, wk_m, wk_t):
    rows = mine.shape[1] + (0 if tail is None else tail.shape[1])
    whole = pl.BlockSpec((rows, HD), lambda i, c: (0, 0))
    wk_spec = pl.BlockSpec((KVS, 2 * PER * FS), lambda i, c: (0, i))
    return pl.pallas_call(
        functools.partial(kv_kernel, tail is not None),
        grid_spec=pltpu.PrefetchScalarGridSpec(
            num_scalar_prefetch=1,
            grid=(STEPS,),
            in_specs=x_specs(mine, tail) + [wk_spec, wk_spec],
            out_specs=[whole, whole],
            scratch_shapes=[pltpu.VMEM((rows, HD), jnp.float32), pltpu.VMEM((rows, HD), jnp.float32)],
        ),
        out_shape=[
            jax.ShapeDtypeStruct((rows, HD), jnp.bfloat16),
            jax.ShapeDtypeStruct((rows, HD), jnp.float32),
        ],
        compiler_params=pltpu.CompilerParams(vmem_limit_bytes=VMEM),
        cost_estimate=pl.CostEstimate(
            flops=2 * rows * D * HD, bytes_accessed=2 * D * (rows + HD), transcendentals=rows
        ),
        name="project_kv",
    )(core, mine, theirs, *([] if tail is None else [tail]), gain, wk_m, wk_t)


def project_q(core, mine, theirs, tail, gain, wq, inverse, lengths):
    rows = inverse.shape[0]
    wq4 = wq.reshape(NZ, 2, FS, FS)
    whole = lambda i, c: (0, 0)
    cos_t, sin_t = rope_tables()
    return pl.pallas_call(
        functools.partial(q_kernel, tail is not None),
        grid_spec=pltpu.PrefetchScalarGridSpec(
            num_scalar_prefetch=1,
            grid=(STEPS,),
            in_specs=x_specs(mine, tail)
            + [
                pl.BlockSpec((PER, 1, FS, FS), lambda i, c: (i, c[0], 0, 0)),
                pl.BlockSpec((PER, 1, FS, FS), lambda i, c: (i, 1 - c[0], 0, 0)),
                pl.BlockSpec((rows, HD), whole),
                pl.BlockSpec((RPS, RPS), whole),
                pl.BlockSpec((MAXLEN, HD), whole),
                pl.BlockSpec((MAXLEN, HD), whole),
            ],
            out_specs=[
                pl.BlockSpec((rows, FS), whole),
                pl.BlockSpec((rows, HD), whole),
                pl.BlockSpec((rows, HD), whole),
                pl.BlockSpec((rows, rows), whole),
            ],
            scratch_shapes=[pltpu.VMEM((rows, FS), jnp.float32)],
        ),
        out_shape=[
            jax.ShapeDtypeStruct((rows, FS), jnp.bfloat16),
            jax.ShapeDtypeStruct((rows, HD), jnp.float32),
            jax.ShapeDtypeStruct((rows, HD), jnp.float32),
            jax.ShapeDtypeStruct((rows, rows), jnp.float32),
        ],
        compiler_params=pltpu.CompilerParams(vmem_limit_bytes=VMEM),
        cost_estimate=pl.CostEstimate(
            flops=2 * rows * D * FS, bytes_accessed=2 * D * (rows + FS), transcendentals=0
        ),
        name="project_q",
    )(core, mine, theirs, *([] if tail is None else [tail]), gain, wq4, wq4, inverse,
      lengths, cos_t, sin_t)


def attention_kernel(core, q_ref, first, second, cos_ref, sin_ref, bias_ref, out_ref):
    one, two = first[...].astype(jnp.float32), second[...].astype(jnp.float32)
    swapped = core[2] == 1
    keys = jnp.where(swapped, two, one)
    values = jnp.where(swapped, one, two).astype(jnp.bfloat16)
    k_rot = turn(keys, cos_ref[...], sin_ref[...])
    for h in range(2):
        scores = lax.dot_general(
            q_ref[:, h * HD : (h + 1) * HD], k_rot, (((1,), (1,)), ((), ())), preferred_element_type=jnp.float32
        )
        masked = scores * (1 / math.sqrt(HD)) + bias_ref[...]
        exponent = jnp.exp(masked - jnp.max(masked, axis=1, keepdims=True))
        weights = (exponent / jnp.sum(exponent, axis=1, keepdims=True)).astype(jnp.bfloat16)
        context = jnp.dot(weights, values, preferred_element_type=jnp.float32)
        out_ref[:, h * HD : (h + 1) * HD] = context.astype(jnp.bfloat16)


def attend(core, q, first, second, cosine, sine, bias):
    rows = q.shape[0]
    vm = pl.BlockSpec(memory_space=pltpu.VMEM)
    return pl.pallas_call(
        attention_kernel,
        in_specs=[pl.BlockSpec(memory_space=pltpu.SMEM)] + [vm] * 6,
        out_specs=vm,
        out_shape=jax.ShapeDtypeStruct((rows, FS), jnp.bfloat16),
        compiler_params=pltpu.CompilerParams(vmem_limit_bytes=VMEM),
        cost_estimate=pl.CostEstimate(
            flops=8 * rows * rows * HD, bytes_accessed=4 * rows * FS, transcendentals=2 * rows * rows
        ),
        name="attend",
    )(core, q, first, second, cosine, sine, bias)


def out_kernel(place, mine, theirs, *rest):
    w_mine, w_theirs, outs = rest[:FAR], rest[FAR : 2 * FAR], rest[2 * FAR :]
    for at, out in enumerate(outs):

        @pl.when(pl.program_id(0) == at)
        def _():
            for k in range(FAR):
                total = jnp.dot(mine[...], w_mine[k][...], preferred_element_type=jnp.float32)
                total += jnp.dot(theirs[...], w_theirs[k][...], preferred_element_type=jnp.float32)
                out[k] = total.astype(jnp.bfloat16)


def out_project(place, mine, theirs, w_mine, w_theirs, shifts):
    rows = mine.shape[0]
    context = pl.BlockSpec((rows, FS), lambda i, p: (0, 0))
    first = shifts[0]
    weights = [
        pl.BlockSpec((FS, FS), lambda i, p, k=k: (0, 2 * (3 * k + lax.rem(p[1] + first + i, 3)) + p[0]))
        for k in range(FAR)
    ]
    return pl.pallas_call(
        out_kernel,
        grid_spec=pltpu.PrefetchScalarGridSpec(
            num_scalar_prefetch=1,
            grid=(len(shifts),),
            in_specs=[context, context] + weights + weights,
            out_specs=[pl.BlockSpec((FAR, rows, FS), lambda i, p: (0, 0, 0))] * len(shifts),
        ),
        out_shape=[jax.ShapeDtypeStruct((FAR, rows, FS), jnp.bfloat16)] * len(shifts),
        compiler_params=pltpu.CompilerParams(vmem_limit_bytes=VMEM),
        cost_estimate=pl.CostEstimate(
            flops=len(shifts) * 4 * rows * FS * FAR * FS,
            bytes_accessed=len(shifts) * 2 * FAR * FS * (rows + 2 * FS),
            transcendentals=0,
        ),
        name="out_project",
    )(place, mine, theirs, *[w_mine] * FAR, *[w_theirs] * FAR)


def sum_over_chips(place, context, theirs, w_mine, w_theirs):
    up, down = out_project(place, context, theirs, w_mine, w_theirs, (1, 2))
    below = lax.ppermute(up, "tensor", [(t, (t + 2) % NT) for t in range(NT)])
    above = lax.ppermute(down, "tensor", [(t, (t - 2) % NT) for t in range(NT)])
    (own,) = out_project(place, context, theirs, w_mine, w_theirs, (0,))
    three = own.astype(jnp.float32) + below.astype(jnp.float32) + above.astype(jnp.float32)
    parts = lax.all_to_all(
        three.astype(jnp.bfloat16), "tensor", split_axis=0, concat_axis=0, tiled=True,
        axis_index_groups=FAR_GROUPS,
    )
    return jnp.sum(parts.astype(jnp.float32), axis=0)


def gather_rows(x):
    rows = x.shape[0]
    tail = None
    if rows > AG_ROWS:
        last = jnp.broadcast_to(x[AG_ROWS:][None], (NT, rows - AG_ROWS, FS))
        tail = lax.all_to_all(last, "tensor", split_axis=0, concat_axis=0, tiled=True)
    return lax.all_gather(x[:AG_ROWS], "tensor", axis=0, axis_index_groups=Z_GROUPS), tail


def layer(rows, rollout, lengths, packing, norm_gain, query_weight, keyval_weight, out_weight):
    source = lax.axis_index("dp")
    tensor_index = lax.axis_index("tensor")
    core = jnp.stack([tensor_index % 2, tensor_index // 2 % 3, tensor_index // 2 % 2, source]).astype(jnp.int32)
    x = rollout[:rows]

    mine, tail = gather_rows(x)
    if tail is not None:
        mine, tail = lax.optimization_barrier((mine, tail))
    theirs = swap(mine)
    gain = norm_gain.reshape(NT, 1, FS)
    wk = keyval_weight.T
    keyval, inverse = project_kv(core, mine, theirs, tail, gain, wk, swap(wk))
    first = lax.ppermute(keyval, "tensor", kv_pairs(True))
    second = lax.ppermute(keyval, "tensor", kv_pairs(False))
    q, cosine, sine, bias = project_q(core, mine, theirs, tail, gain, query_weight, inverse, lengths)
    context = attend(core, q, first, second, cosine, sine, bias)
    summed = sum_over_chips(core, context, swap(context), out_weight, swap(out_weight))
    my_len = lax.dynamic_index_in_dim(lengths, source, 0, keepdims=False)
    earlier = jnp.arange(RPS)[None, :] < jnp.arange(RPS)[:, None]
    start = jnp.sum(jnp.where(earlier, my_len[None, :], 0), axis=1)
    places = jnp.arange(rows, dtype=jnp.int32)
    result = (summed + x.astype(jnp.float32)).astype(jnp.bfloat16)

    pack = packing.reshape(RPS, RPS)
    of_mine = pack // RPS == source
    which = jnp.sum(jnp.where(of_mine, pack % RPS, 0), axis=1)
    chosen = which[:, None] == jnp.arange(RPS)[None, :]
    o_start = jnp.sum(jnp.where(chosen, start[None, :], 0), axis=1)
    o_len = jnp.sum(jnp.where(chosen, my_len[None, :], 0), axis=1)
    slot = jnp.arange(MAXLEN, dtype=jnp.int32)
    row_of = jnp.where(slot[None, :] < o_len[:, None], o_start[:, None] + slot[None, :], -1).reshape(-1)
    pick = (row_of[:, None] == places[None, :]).astype(jnp.bfloat16)
    outgoing = jnp.dot(pick, result, preferred_element_type=jnp.float32).astype(jnp.bfloat16)
    return outgoing


def body(rollout, lengths, packing, norm_gain, query_weight, keyval_weight, out_weight):
    owner = lax.axis_index("dp")
    total = rollout.shape[0]
    longest = jnp.max(jnp.sum(lengths, axis=1))
    size = sum((longest > cap).astype(jnp.int32) for cap in CAPS[:-1])
    outgoing = lax.switch(
        size,
        [functools.partial(layer, cap) for cap in CAPS],
        rollout, lengths, packing, norm_gain, query_weight, keyval_weight, out_weight,
    )
    incoming = lax.all_to_all(
        outgoing.reshape(RPS, MAXLEN, FS), "dp", split_axis=0, concat_axis=0, tiled=True
    ).reshape(RPS * MAXLEN, FS)

    chosen = lax.dynamic_index_in_dim(packing.reshape(RPS, RPS), owner, 0, keepdims=False)
    from_source = chosen // RPS
    is_source = from_source[:, None] == jnp.arange(RPS)[None, :]
    of_source = jnp.sum(jnp.where(is_source[:, :, None], lengths[None], 0), axis=1)
    is_k = (chosen % RPS)[:, None] == jnp.arange(RPS)[None, :]
    length = jnp.sum(jnp.where(is_k, of_source, 0), axis=1)
    earlier = jnp.arange(RPS)[None, :] < jnp.arange(RPS)[:, None]
    start = jnp.sum(jnp.where(earlier, length[None, :], 0), axis=1)
    places = jnp.arange(total, dtype=jnp.int32)
    inside = (places[:, None] >= start[None, :]) & (places[:, None] < (start + length)[None, :])
    valid = jnp.any(inside, axis=1)
    at = jnp.sum(jnp.where(inside, from_source[None, :] * MAXLEN + places[:, None] - start[None, :], 0), axis=1)
    at = jnp.where(valid, at, -1)
    pick = (at[:, None] == jnp.arange(RPS * MAXLEN)[None, :]).astype(jnp.bfloat16)
    return jnp.dot(pick, incoming, preferred_element_type=jnp.float32).astype(jnp.bfloat16)


def solution(mesh):
    in_specs = (
        P("dp", "tensor"),
        P(),
        P(),
        P(),
        P(None, "tensor"),
        P(None, "tensor"),
        P("tensor", None),
    )
    out_specs = P("dp", "tensor")
    return jax.shard_map(body, mesh=mesh, in_specs=in_specs, out_specs=out_specs, check_vma=False)
```

```python
import functools
import math

import jax
import jax.numpy as jnp
import numpy as np
from jax import lax
from jax.experimental import pallas as pl
from jax.experimental.pallas import tpu as pltpu
from jax.sharding import PartitionSpec as P

D = 6144
HD = 128
MAXLEN = 8
NZ = 12
NT = 24
FS = 256
RPS = 32
KVS = 64
EPS = 1e-05
ROPE_BASE = 500000.0
AG_ROWS = 168
VMEM = 24 * 1024 * 1024

Z_GROUPS = [[z * 2 + c for z in range(NZ)] for c in range(2)]
FAR = 4
FAR_GROUPS = [[(3 * k + r) * 2 + c for k in range(FAR)] for r in range(3) for c in range(2)]
SWAP = [(t, t ^ 1) for t in range(NT)]


STEPS = 3
PER = NZ // STEPS
CAPS = (168, 176, 192, 256)


def rope_tables():
    frequency = ROPE_BASE ** (-np.arange(HD // 2) * 2.0 / HD)
    angles = np.arange(MAXLEN)[:, None] * np.concatenate([frequency, frequency])[None, :]
    sign = np.where(np.arange(HD) < HD // 2, -1.0, 1.0)[None, :]
    return np.cos(angles).astype(np.float32), (np.sin(angles) * sign).astype(np.float32)


def turn(v, cosine, sine):
    turned = jnp.concatenate([v[:, HD // 2 :], v[:, : HD // 2]], axis=1)
    return (v * cosine + turned * sine).astype(jnp.bfloat16)


def documents(lengths, source, rows):
    own = lengths[pl.ds(source, 1), :].astype(jnp.float32)
    first = lax.broadcasted_iota(jnp.int32, (RPS, RPS), 0)
    second = lax.broadcasted_iota(jnp.int32, (RPS, RPS), 1)
    column = jnp.sum(jnp.where(first == second, own, 0.0), axis=1, keepdims=True)
    end = jnp.sum(jnp.where(first <= second, column, 0.0), axis=0, keepdims=True)
    end_column = jnp.sum(jnp.where(second <= first, own, 0.0), axis=1, keepdims=True)
    start = end - own
    place = lax.broadcasted_iota(jnp.int32, (rows, RPS), 0).astype(jnp.float32)
    doc = jnp.sum(jnp.where(place >= end, 1.0, 0.0), axis=1, keepdims=True)
    begun = jnp.max(jnp.where(start <= place, start, 0.0), axis=1, keepdims=True)
    position = jnp.where(doc < RPS, place[:, :1] - begun, 0.0)
    along = lax.broadcasted_iota(jnp.int32, (RPS, rows), 1).astype(jnp.float32)
    doc_row = jnp.sum(jnp.where(along >= end_column, 1.0, 0.0), axis=0, keepdims=True)
    return doc, position, doc_row


def kv_pairs(first):
    pairs = []
    for z in range(NZ):
        g, value = z % (NZ // 2), z // (NZ // 2)
        to = 2 * g + (value if first else 1 - value)
        pairs += [(2 * z + c, 2 * to + c) for c in range(2)]
    return pairs


def swap(v):
    return lax.ppermute(v, "tensor", SWAP)


def rows_of(refs, j, side):
    head, tail = refs
    x = head[j].astype(jnp.float32)
    if tail is not None:
        x = jnp.concatenate([x, tail[2 * j + side].astype(jnp.float32)], axis=0)
    return x


def kv_kernel(has_tail, core, mine, *rest):
    if has_tail:
        tail, *rest = rest
    else:
        tail = None
    gain, wk_m, wk_t, out, kv_acc, sq_acc = rest
    step = pl.program_id(0)
    c = core[0]

    @pl.when(step == 0)
    def _():
        kv_acc[...] = jnp.zeros_like(kv_acc)
        sq_acc[...] = jnp.zeros_like(sq_acc)

    total, squares = kv_acc[...], sq_acc[...]
    for j in range(PER):
        x = rows_of((mine, tail), j, c)
        square = x * x
        squares += square[:, :128] + square[:, 128:]
        scaled = (x * gain[2 * j + c]).astype(jnp.bfloat16)
        at = pl.ds(pl.multiple_of((2 * j + c) * FS, FS), FS)
        w = jnp.concatenate([wk_m[:, at], wk_t[:, at]], axis=0)
        total += lax.dot_general(scaled, w, (((1,), (1,)), ((), ())), preferred_element_type=jnp.float32)
    kv_acc[...] = total
    sq_acc[...] = squares

    @pl.when(step == STEPS - 1)
    def _():
        turned = jnp.concatenate([total[:, KVS:], total[:, :KVS]], axis=1)
        out[:, :HD] = jnp.where(c == 0, total, turned)
        out[:, HD:] = squares


def join_kernel(mine, theirs, kv_out, inv_out):
    total = mine[...] + theirs[...]
    inverse = lax.rsqrt(jnp.sum(total[:, HD:], axis=1, keepdims=True) / D + EPS)
    kv_out[...] = (total[:, :HD] * inverse).astype(jnp.bfloat16)
    inv_out[...] = jnp.broadcast_to(inverse, inv_out.shape)


def q_kernel(has_tail, core, mine, theirs, *rest):
    if has_tail:
        tail, *rest = rest
    else:
        tail = None
    gain, wq_m, wq_t, inv, lengths, cos_t, sin_t, q_out, cos_out, sin_out, bias_out, q_acc = rest
    step = pl.program_id(0)
    c = core[0]
    rows = q_acc.shape[0]

    @pl.when(step == 0)
    def _():
        q_acc[...] = jnp.zeros_like(q_acc)
        doc, position, doc_row = documents(lengths, core[3], rows)
        cosine = jnp.broadcast_to(cos_t[0:1], (rows, HD))
        sine = jnp.broadcast_to(sin_t[0:1], (rows, HD))
        for m in range(1, MAXLEN):
            here = jnp.broadcast_to(position == m, (rows, HD))
            cosine = jnp.where(here, cos_t[m : m + 1], cosine)
            sine = jnp.where(here, sin_t[m : m + 1], sine)
        cos_out[...] = cosine
        sin_out[...] = sine
        place_q = lax.broadcasted_iota(jnp.int32, (rows, rows), 0)
        place_k = lax.broadcasted_iota(jnp.int32, (rows, rows), 1)
        allowed = (doc == doc_row) & (place_k <= place_q)
        bias_out[...] = jnp.where(allowed, 0.0, -jnp.inf)

    total = q_acc[...]
    for j in range(PER):
        for x_ref, wq, side in ((mine, wq_m, c), (theirs, wq_t, 1 - c)):
            x = rows_of((x_ref, tail), j, side)
            scaled = (x * gain[2 * j + side]).astype(jnp.bfloat16)
            total += jnp.dot(scaled, wq[j, 0], preferred_element_type=jnp.float32)
    q_acc[...] = total

    @pl.when(step == STEPS - 1)
    def _():
        for h in range(2):
            head = total[:, h * HD : (h + 1) * HD] * inv[...]
            q_out[:, h * HD : (h + 1) * HD] = turn(head, cos_out[...], sin_out[...])


def x_specs(xs, tail):
    specs = [pl.BlockSpec((PER, x.shape[1], FS), lambda i, c: (i, 0, 0)) for x in xs]
    if tail is not None:
        specs.append(pl.BlockSpec((2 * PER, tail.shape[1], FS), lambda i, c: (i, 0, 0)))
    specs.append(pl.BlockSpec((2 * PER, 1, FS), lambda i, c: (i, 0, 0)))
    return specs


def project_kv(core, mine, tail, gain, wk_m, wk_t):
    rows = mine.shape[1] + (0 if tail is None else tail.shape[1])
    wk_spec = pl.BlockSpec((KVS, 2 * PER * FS), lambda i, c: (0, i))
    part = pl.pallas_call(
        functools.partial(kv_kernel, tail is not None),
        grid_spec=pltpu.PrefetchScalarGridSpec(
            num_scalar_prefetch=1,
            grid=(STEPS,),
            in_specs=x_specs([mine], tail) + [wk_spec, wk_spec],
            out_specs=pl.BlockSpec((rows, 2 * HD), lambda i, c: (0, 0)),
            scratch_shapes=[pltpu.VMEM((rows, HD), jnp.float32), pltpu.VMEM((rows, HD), jnp.float32)],
        ),
        out_shape=jax.ShapeDtypeStruct((rows, 2 * HD), jnp.float32),
        compiler_params=pltpu.CompilerParams(vmem_limit_bytes=VMEM),
        cost_estimate=pl.CostEstimate(
            flops=rows * D * HD, bytes_accessed=D * (rows + 2 * HD), transcendentals=0
        ),
        name="project_kv",
    )(core, mine, *([] if tail is None else [tail]), gain, wk_m, wk_t)
    vm = pl.BlockSpec(memory_space=pltpu.VMEM)
    return pl.pallas_call(
        join_kernel,
        in_specs=[vm, vm],
        out_specs=[vm, vm],
        out_shape=[
            jax.ShapeDtypeStruct((rows, HD), jnp.bfloat16),
            jax.ShapeDtypeStruct((rows, HD), jnp.float32),
        ],
        compiler_params=pltpu.CompilerParams(vmem_limit_bytes=VMEM),
        name="join_kv",
    )(part, swap(part))


def project_q(core, mine, theirs, tail, gain, wq, inverse, lengths):
    rows = inverse.shape[0]
    wq4 = wq.reshape(NZ, 2, FS, FS)
    whole = lambda i, c: (0, 0)
    cos_t, sin_t = rope_tables()
    return pl.pallas_call(
        functools.partial(q_kernel, tail is not None),
        grid_spec=pltpu.PrefetchScalarGridSpec(
            num_scalar_prefetch=1,
            grid=(STEPS,),
            in_specs=x_specs([mine, theirs], tail)
            + [
                pl.BlockSpec((PER, 1, FS, FS), lambda i, c: (i, c[0], 0, 0)),
                pl.BlockSpec((PER, 1, FS, FS), lambda i, c: (i, 1 - c[0], 0, 0)),
                pl.BlockSpec((rows, HD), whole),
                pl.BlockSpec((RPS, RPS), whole),
                pl.BlockSpec((MAXLEN, HD), whole),
                pl.BlockSpec((MAXLEN, HD), whole),
            ],
            out_specs=[
                pl.BlockSpec((rows, FS), whole),
                pl.BlockSpec((rows, HD), whole),
                pl.BlockSpec((rows, HD), whole),
                pl.BlockSpec((rows, rows), whole),
            ],
            scratch_shapes=[pltpu.VMEM((rows, FS), jnp.float32)],
        ),
        out_shape=[
            jax.ShapeDtypeStruct((rows, FS), jnp.bfloat16),
            jax.ShapeDtypeStruct((rows, HD), jnp.float32),
            jax.ShapeDtypeStruct((rows, HD), jnp.float32),
            jax.ShapeDtypeStruct((rows, rows), jnp.float32),
        ],
        compiler_params=pltpu.CompilerParams(vmem_limit_bytes=VMEM),
        cost_estimate=pl.CostEstimate(
            flops=2 * rows * D * FS, bytes_accessed=2 * D * (rows + FS), transcendentals=0
        ),
        name="project_q",
    )(core, mine, theirs, *([] if tail is None else [tail]), gain, wq4, wq4, inverse,
      lengths, cos_t, sin_t)


def attention_kernel(core, q_ref, first, second, cos_ref, sin_ref, bias_ref, out_ref):
    one, two = first[...].astype(jnp.float32), second[...].astype(jnp.float32)
    swapped = core[2] == 1
    keys = jnp.where(swapped, two, one)
    values = jnp.where(swapped, one, two).astype(jnp.bfloat16)
    k_rot = turn(keys, cos_ref[...], sin_ref[...])
    for h in range(2):
        scores = lax.dot_general(
            q_ref[:, h * HD : (h + 1) * HD], k_rot, (((1,), (1,)), ((), ())), preferred_element_type=jnp.float32
        )
        masked = scores * (1 / math.sqrt(HD)) + bias_ref[...]
        exponent = jnp.exp(masked - jnp.max(masked, axis=1, keepdims=True))
        weights = (exponent / jnp.sum(exponent, axis=1, keepdims=True)).astype(jnp.bfloat16)
        context = jnp.dot(weights, values, preferred_element_type=jnp.float32)
        out_ref[:, h * HD : (h + 1) * HD] = context.astype(jnp.bfloat16)


def attend(core, q, first, second, cosine, sine, bias):
    rows = q.shape[0]
    vm = pl.BlockSpec(memory_space=pltpu.VMEM)
    return pl.pallas_call(
        attention_kernel,
        in_specs=[pl.BlockSpec(memory_space=pltpu.SMEM)] + [vm] * 6,
        out_specs=vm,
        out_shape=jax.ShapeDtypeStruct((rows, FS), jnp.bfloat16),
        compiler_params=pltpu.CompilerParams(vmem_limit_bytes=VMEM),
        cost_estimate=pl.CostEstimate(
            flops=8 * rows * rows * HD, bytes_accessed=4 * rows * FS, transcendentals=2 * rows * rows
        ),
        name="attend",
    )(core, q, first, second, cosine, sine, bias)


def out_kernel(place, mine, theirs, *rest):
    w_mine, w_theirs, outs = rest[:FAR], rest[FAR : 2 * FAR], rest[2 * FAR :]
    for at, out in enumerate(outs):

        @pl.when(pl.program_id(0) == at)
        def _():
            for k in range(FAR):
                total = jnp.dot(mine[...], w_mine[k][...], preferred_element_type=jnp.float32)
                total += jnp.dot(theirs[...], w_theirs[k][...], preferred_element_type=jnp.float32)
                out[k] = total.astype(jnp.bfloat16)


def out_project(place, mine, theirs, w_mine, w_theirs, shifts):
    rows = mine.shape[0]
    context = pl.BlockSpec((rows, FS), lambda i, p: (0, 0))
    first = shifts[0]
    weights = [
        pl.BlockSpec((FS, FS), lambda i, p, k=k: (0, 2 * (3 * k + lax.rem(p[1] + first + i, 3)) + p[0]))
        for k in range(FAR)
    ]
    return pl.pallas_call(
        out_kernel,
        grid_spec=pltpu.PrefetchScalarGridSpec(
            num_scalar_prefetch=1,
            grid=(len(shifts),),
            in_specs=[context, context] + weights + weights,
            out_specs=[pl.BlockSpec((FAR, rows, FS), lambda i, p: (0, 0, 0))] * len(shifts),
        ),
        out_shape=[jax.ShapeDtypeStruct((FAR, rows, FS), jnp.bfloat16)] * len(shifts),
        compiler_params=pltpu.CompilerParams(vmem_limit_bytes=VMEM),
        cost_estimate=pl.CostEstimate(
            flops=len(shifts) * 4 * rows * FS * FAR * FS,
            bytes_accessed=len(shifts) * 2 * FAR * FS * (rows + 2 * FS),
            transcendentals=0,
        ),
        name="out_project",
    )(place, mine, theirs, *[w_mine] * FAR, *[w_theirs] * FAR)


def sum_over_chips(place, context, theirs, w_mine, w_theirs):
    up, down = out_project(place, context, theirs, w_mine, w_theirs, (1, 2))
    below = lax.ppermute(up, "tensor", [(t, (t + 2) % NT) for t in range(NT)])
    above = lax.ppermute(down, "tensor", [(t, (t - 2) % NT) for t in range(NT)])
    (own,) = out_project(place, context, theirs, w_mine, w_theirs, (0,))
    three = own.astype(jnp.float32) + below.astype(jnp.float32) + above.astype(jnp.float32)
    parts = lax.all_to_all(
        three.astype(jnp.bfloat16), "tensor", split_axis=0, concat_axis=0, tiled=True,
        axis_index_groups=FAR_GROUPS,
    )
    return jnp.sum(parts.astype(jnp.float32), axis=0)


def gather_rows(x):
    rows = x.shape[0]
    tail = None
    if rows > AG_ROWS:
        last = jnp.broadcast_to(x[AG_ROWS:][None], (NT, rows - AG_ROWS, FS))
        tail = lax.all_to_all(last, "tensor", split_axis=0, concat_axis=0, tiled=True)
    return lax.all_gather(x[:AG_ROWS], "tensor", axis=0, axis_index_groups=Z_GROUPS), tail


def layer(rows, rollout, lengths, packing, norm_gain, query_weight, keyval_weight, out_weight):
    source = lax.axis_index("dp")
    tensor_index = lax.axis_index("tensor")
    core = jnp.stack([tensor_index % 2, tensor_index // 2 % 3, tensor_index // 2 % 2, source]).astype(jnp.int32)
    x = rollout[:rows]

    mine, tail = gather_rows(x)
    gain = norm_gain.reshape(NT, 1, FS)
    wk = keyval_weight.T
    mine, tail, wk_theirs = lax.optimization_barrier((mine, tail, swap(wk)))
    theirs = swap(mine)
    keyval, inverse = project_kv(core, mine, tail, gain, wk, wk_theirs)
    first = lax.ppermute(keyval, "tensor", kv_pairs(True))
    second = lax.ppermute(keyval, "tensor", kv_pairs(False))
    q, cosine, sine, bias = project_q(core, mine, theirs, tail, gain, query_weight, inverse, lengths)
    context = attend(core, q, first, second, cosine, sine, bias)
    summed = sum_over_chips(core, context, swap(context), out_weight, swap(out_weight))
    my_len = lax.dynamic_index_in_dim(lengths, source, 0, keepdims=False)
    earlier = jnp.arange(RPS)[None, :] < jnp.arange(RPS)[:, None]
    start = jnp.sum(jnp.where(earlier, my_len[None, :], 0), axis=1)
    places = jnp.arange(rows, dtype=jnp.int32)
    result = (summed + x.astype(jnp.float32)).astype(jnp.bfloat16)

    pack = packing.reshape(RPS, RPS)
    of_mine = pack // RPS == source
    which = jnp.sum(jnp.where(of_mine, pack % RPS, 0), axis=1)
    chosen = which[:, None] == jnp.arange(RPS)[None, :]
    o_start = jnp.sum(jnp.where(chosen, start[None, :], 0), axis=1)
    o_len = jnp.sum(jnp.where(chosen, my_len[None, :], 0), axis=1)
    slot = jnp.arange(MAXLEN, dtype=jnp.int32)
    row_of = jnp.where(slot[None, :] < o_len[:, None], o_start[:, None] + slot[None, :], -1).reshape(-1)
    pick = (row_of[:, None] == places[None, :]).astype(jnp.bfloat16)
    outgoing = jnp.dot(pick, result, preferred_element_type=jnp.float32).astype(jnp.bfloat16)
    return outgoing


def body(rollout, lengths, packing, norm_gain, query_weight, keyval_weight, out_weight):
    owner = lax.axis_index("dp")
    total = rollout.shape[0]
    longest = jnp.max(jnp.sum(lengths, axis=1))
    size = sum((longest > cap).astype(jnp.int32) for cap in CAPS[:-1])
    outgoing = lax.switch(
        size,
        [functools.partial(layer, cap) for cap in CAPS],
        rollout, lengths, packing, norm_gain, query_weight, keyval_weight, out_weight,
    )
    incoming = lax.all_to_all(
        outgoing.reshape(RPS, MAXLEN, FS), "dp", split_axis=0, concat_axis=0, tiled=True
    ).reshape(RPS * MAXLEN, FS)

    chosen = lax.dynamic_index_in_dim(packing.reshape(RPS, RPS), owner, 0, keepdims=False)
    from_source = chosen // RPS
    is_source = from_source[:, None] == jnp.arange(RPS)[None, :]
    of_source = jnp.sum(jnp.where(is_source[:, :, None], lengths[None], 0), axis=1)
    is_k = (chosen % RPS)[:, None] == jnp.arange(RPS)[None, :]
    length = jnp.sum(jnp.where(is_k, of_source, 0), axis=1)
    earlier = jnp.arange(RPS)[None, :] < jnp.arange(RPS)[:, None]
    start = jnp.sum(jnp.where(earlier, length[None, :], 0), axis=1)
    places = jnp.arange(total, dtype=jnp.int32)
    inside = (places[:, None] >= start[None, :]) & (places[:, None] < (start + length)[None, :])
    valid = jnp.any(inside, axis=1)
    at = jnp.sum(jnp.where(inside, from_source[None, :] * MAXLEN + places[:, None] - start[None, :], 0), axis=1)
    at = jnp.where(valid, at, -1)
    pick = (at[:, None] == jnp.arange(RPS * MAXLEN)[None, :]).astype(jnp.bfloat16)
    return jnp.dot(pick, incoming, preferred_element_type=jnp.float32).astype(jnp.bfloat16)


def solution(mesh):
    in_specs = (
        P("dp", "tensor"),
        P(),
        P(),
        P(),
        P(None, "tensor"),
        P(None, "tensor"),
        P("tensor", None),
    )
    out_specs = P("dp", "tensor")
    return jax.shard_map(body, mesh=mesh, in_specs=in_specs, out_specs=out_specs, check_vma=False)
```

```python
import functools
import math

import jax
import jax.numpy as jnp
import numpy as np
from jax import lax
from jax.experimental import pallas as pl
from jax.experimental.pallas import tpu as pltpu
from jax.sharding import PartitionSpec as P

D = 6144
HD = 128
MAXLEN = 8
NZ = 12
NT = 24
FS = 256
RPS = 32
KVS = 64
EPS = 1e-05
ROPE_BASE = 500000.0
AG_ROWS = 168
VMEM = 24 * 1024 * 1024

Z_GROUPS = [[z * 2 + c for z in range(NZ)] for c in range(2)]
FAR = 4
FAR_GROUPS = [[(3 * k + r) * 2 + c for k in range(FAR)] for r in range(3) for c in range(2)]
SWAP = [(t, t ^ 1) for t in range(NT)]


STEPS = 3
PER = NZ // STEPS
CAPS = (168, 176, 192, 256)


def rope_tables():
    frequency = ROPE_BASE ** (-np.arange(HD // 2) * 2.0 / HD)
    angles = np.arange(MAXLEN)[:, None] * np.concatenate([frequency, frequency])[None, :]
    sign = np.where(np.arange(HD) < HD // 2, -1.0, 1.0)[None, :]
    return np.cos(angles).astype(np.float32), (np.sin(angles) * sign).astype(np.float32)


def turn(v, cosine, sine):
    turned = jnp.concatenate([v[:, HD // 2 :], v[:, : HD // 2]], axis=1)
    return (v * cosine + turned * sine).astype(jnp.bfloat16)


def documents(lengths, source, rows):
    own = lengths[pl.ds(source, 1), :].astype(jnp.float32)
    first = lax.broadcasted_iota(jnp.int32, (RPS, RPS), 0)
    second = lax.broadcasted_iota(jnp.int32, (RPS, RPS), 1)
    column = jnp.sum(jnp.where(first == second, own, 0.0), axis=1, keepdims=True)
    end = jnp.sum(jnp.where(first <= second, column, 0.0), axis=0, keepdims=True)
    end_column = jnp.sum(jnp.where(second <= first, own, 0.0), axis=1, keepdims=True)
    start = end - own
    place = lax.broadcasted_iota(jnp.int32, (rows, RPS), 0).astype(jnp.float32)
    doc = jnp.sum(jnp.where(place >= end, 1.0, 0.0), axis=1, keepdims=True)
    begun = jnp.max(jnp.where(start <= place, start, 0.0), axis=1, keepdims=True)
    position = jnp.where(doc < RPS, place[:, :1] - begun, 0.0)
    along = lax.broadcasted_iota(jnp.int32, (RPS, rows), 1).astype(jnp.float32)
    doc_row = jnp.sum(jnp.where(along >= end_column, 1.0, 0.0), axis=0, keepdims=True)
    return doc, position, doc_row


def kv_pairs(first):
    pairs = []
    for z in range(NZ):
        g, value = z % (NZ // 2), z // (NZ // 2)
        to = 2 * g + (value if first else 1 - value)
        pairs += [(2 * z + c, 2 * to + c) for c in range(2)]
    return pairs


def swap(v):
    return lax.ppermute(v, "tensor", SWAP)


def rows_of(refs, j, side):
    head, tail = refs
    x = head[j].astype(jnp.float32)
    if tail is not None:
        x = jnp.concatenate([x, tail[2 * j + side].astype(jnp.float32)], axis=0)
    return x


def kv_kernel(has_tail, core, mine, *rest):
    if has_tail:
        tail, *rest = rest
    else:
        tail = None
    gain, wk_m, wk_t, out, kv_acc, sq_acc = rest
    step = pl.program_id(0)
    c = core[0]

    @pl.when(step == 0)
    def _():
        kv_acc[...] = jnp.zeros_like(kv_acc)
        sq_acc[...] = jnp.zeros_like(sq_acc)

    total, squares = kv_acc[...], sq_acc[...]
    for j in range(PER):
        x = rows_of((mine, tail), j, c)
        square = x * x
        squares += square[:, :128] + square[:, 128:]
        scaled = (x * gain[2 * j + c]).astype(jnp.bfloat16)
        at = pl.ds(pl.multiple_of((2 * j + c) * FS, FS), FS)
        w = jnp.concatenate([wk_m[:, at], wk_t[:, at]], axis=0)
        total += lax.dot_general(scaled, w, (((1,), (1,)), ((), ())), preferred_element_type=jnp.float32)
    kv_acc[...] = total
    sq_acc[...] = squares

    @pl.when(step == STEPS - 1)
    def _():
        turned = jnp.concatenate([total[:, KVS:], total[:, :KVS]], axis=1)
        out[:, :HD] = jnp.where(c == 0, total, turned)
        out[:, HD:] = squares


def join_kernel(mine, theirs, kv_out, inv_out):
    total = mine[...] + theirs[...]
    inverse = lax.rsqrt(jnp.sum(total[:, HD:], axis=1, keepdims=True) / D + EPS)
    kv_out[...] = (total[:, :HD] * inverse).astype(jnp.bfloat16)
    inv_out[...] = jnp.broadcast_to(inverse, inv_out.shape)


def q_kernel(has_tail, core, mine, theirs, *rest):
    if has_tail:
        tail, *rest = rest
    else:
        tail = None
    gain, wq_m, wq_t, inv, lengths, cos_t, sin_t, q_out, cos_out, sin_out, bias_out, q_acc = rest
    step = pl.program_id(0)
    c = core[0]
    rows = q_acc.shape[0]

    @pl.when(step == 0)
    def _():
        q_acc[...] = jnp.zeros_like(q_acc)
        doc, position, doc_row = documents(lengths, core[3], rows)
        cosine = jnp.broadcast_to(cos_t[0:1], (rows, HD))
        sine = jnp.broadcast_to(sin_t[0:1], (rows, HD))
        for m in range(1, MAXLEN):
            here = jnp.broadcast_to(position == m, (rows, HD))
            cosine = jnp.where(here, cos_t[m : m + 1], cosine)
            sine = jnp.where(here, sin_t[m : m + 1], sine)
        cos_out[...] = cosine
        sin_out[...] = sine
        place_q = lax.broadcasted_iota(jnp.int32, (rows, rows), 0)
        place_k = lax.broadcasted_iota(jnp.int32, (rows, rows), 1)
        allowed = (doc == doc_row) & (place_k <= place_q)
        bias_out[...] = jnp.where(allowed, 0.0, -jnp.inf)

    total = q_acc[...]
    for j in range(PER):
        for x_ref, wq, side in ((mine, wq_m, c), (theirs, wq_t, 1 - c)):
            x = rows_of((x_ref, tail), j, side)
            scaled = (x * gain[2 * j + side]).astype(jnp.bfloat16)
            total += jnp.dot(scaled, wq[j, 0], preferred_element_type=jnp.float32)
    q_acc[...] = total

    @pl.when(step == STEPS - 1)
    def _():
        for h in range(2):
            head = total[:, h * HD : (h + 1) * HD] * inv[...]
            q_out[:, h * HD : (h + 1) * HD] = turn(head, cos_out[...], sin_out[...])


def x_specs(xs, tail):
    specs = [pl.BlockSpec((PER, x.shape[1], FS), lambda i, c: (i, 0, 0)) for x in xs]
    if tail is not None:
        specs.append(pl.BlockSpec((2 * PER, tail.shape[1], FS), lambda i, c: (i, 0, 0)))
    specs.append(pl.BlockSpec((2 * PER, 1, FS), lambda i, c: (i, 0, 0)))
    return specs


def project_kv(core, mine, tail, gain, wk_m, wk_t):
    rows = mine.shape[1] + (0 if tail is None else tail.shape[1])
    wk_spec = pl.BlockSpec((KVS, 2 * PER * FS), lambda i, c: (0, i))
    part = pl.pallas_call(
        functools.partial(kv_kernel, tail is not None),
        grid_spec=pltpu.PrefetchScalarGridSpec(
            num_scalar_prefetch=1,
            grid=(STEPS,),
            in_specs=x_specs([mine], tail) + [wk_spec, wk_spec],
            out_specs=pl.BlockSpec((rows, 2 * HD), lambda i, c: (0, 0)),
            scratch_shapes=[pltpu.VMEM((rows, HD), jnp.float32), pltpu.VMEM((rows, HD), jnp.float32)],
        ),
        out_shape=jax.ShapeDtypeStruct((rows, 2 * HD), jnp.float32),
        compiler_params=pltpu.CompilerParams(vmem_limit_bytes=VMEM),
        cost_estimate=pl.CostEstimate(
            flops=rows * D * HD, bytes_accessed=D * (rows + 2 * HD), transcendentals=0
        ),
        name="project_kv",
    )(core, mine, *([] if tail is None else [tail]), gain, wk_m, wk_t)
    vm = pl.BlockSpec(memory_space=pltpu.VMEM)
    return pl.pallas_call(
        join_kernel,
        in_specs=[vm, vm],
        out_specs=[vm, vm],
        out_shape=[
            jax.ShapeDtypeStruct((rows, HD), jnp.bfloat16),
            jax.ShapeDtypeStruct((rows, HD), jnp.float32),
        ],
        compiler_params=pltpu.CompilerParams(vmem_limit_bytes=VMEM),
        name="join_kv",
    )(part, swap(part))


def project_q(core, mine, theirs, tail, gain, wq, inverse, lengths):
    rows = inverse.shape[0]
    wq4 = wq.reshape(NZ, 2, FS, FS)
    whole = lambda i, c: (0, 0)
    cos_t, sin_t = rope_tables()
    return pl.pallas_call(
        functools.partial(q_kernel, tail is not None),
        grid_spec=pltpu.PrefetchScalarGridSpec(
            num_scalar_prefetch=1,
            grid=(STEPS,),
            in_specs=x_specs([mine, theirs], tail)
            + [
                pl.BlockSpec((PER, 1, FS, FS), lambda i, c: (i, c[0], 0, 0)),
                pl.BlockSpec((PER, 1, FS, FS), lambda i, c: (i, 1 - c[0], 0, 0)),
                pl.BlockSpec((rows, HD), whole),
                pl.BlockSpec((RPS, RPS), whole),
                pl.BlockSpec((MAXLEN, HD), whole),
                pl.BlockSpec((MAXLEN, HD), whole),
            ],
            out_specs=[
                pl.BlockSpec((rows, FS), whole),
                pl.BlockSpec((rows, HD), whole),
                pl.BlockSpec((rows, HD), whole),
                pl.BlockSpec((rows, rows), whole),
            ],
            scratch_shapes=[pltpu.VMEM((rows, FS), jnp.float32)],
        ),
        out_shape=[
            jax.ShapeDtypeStruct((rows, FS), jnp.bfloat16),
            jax.ShapeDtypeStruct((rows, HD), jnp.float32),
            jax.ShapeDtypeStruct((rows, HD), jnp.float32),
            jax.ShapeDtypeStruct((rows, rows), jnp.float32),
        ],
        compiler_params=pltpu.CompilerParams(vmem_limit_bytes=VMEM),
        cost_estimate=pl.CostEstimate(
            flops=2 * rows * D * FS, bytes_accessed=2 * D * (rows + FS), transcendentals=0
        ),
        name="project_q",
    )(core, mine, theirs, *([] if tail is None else [tail]), gain, wq4, wq4, inverse,
      lengths, cos_t, sin_t)


def attention_kernel(core, q_ref, first, second, cos_ref, sin_ref, bias_ref, out_ref):
    one, two = first[...].astype(jnp.float32), second[...].astype(jnp.float32)
    swapped = core[2] == 1
    keys = jnp.where(swapped, two, one)
    values = jnp.where(swapped, one, two).astype(jnp.bfloat16)
    k_rot = turn(keys, cos_ref[...], sin_ref[...])
    for h in range(2):
        scores = lax.dot_general(
            q_ref[:, h * HD : (h + 1) * HD], k_rot, (((1,), (1,)), ((), ())), preferred_element_type=jnp.float32
        )
        masked = scores * (1 / math.sqrt(HD)) + bias_ref[...]
        exponent = jnp.exp(masked - jnp.max(masked, axis=1, keepdims=True))
        weights = (exponent / jnp.sum(exponent, axis=1, keepdims=True)).astype(jnp.bfloat16)
        context = jnp.dot(weights, values, preferred_element_type=jnp.float32)
        out_ref[:, h * HD : (h + 1) * HD] = context.astype(jnp.bfloat16)


def attend(core, q, first, second, cosine, sine, bias):
    rows = q.shape[0]
    vm = pl.BlockSpec(memory_space=pltpu.VMEM)
    return pl.pallas_call(
        attention_kernel,
        in_specs=[pl.BlockSpec(memory_space=pltpu.SMEM)] + [vm] * 6,
        out_specs=vm,
        out_shape=jax.ShapeDtypeStruct((rows, FS), jnp.bfloat16),
        compiler_params=pltpu.CompilerParams(vmem_limit_bytes=VMEM),
        cost_estimate=pl.CostEstimate(
            flops=8 * rows * rows * HD, bytes_accessed=4 * rows * FS, transcendentals=2 * rows * rows
        ),
        name="attend",
    )(core, q, first, second, cosine, sine, bias)


def out_kernel(place, mine, theirs, *rest):
    w_mine, w_theirs, outs = rest[:FAR], rest[FAR : 2 * FAR], rest[2 * FAR :]
    for at, out in enumerate(outs):

        @pl.when(pl.program_id(0) == at)
        def _():
            for k in range(FAR):
                total = jnp.dot(mine[...], w_mine[k][...], preferred_element_type=jnp.float32)
                total += jnp.dot(theirs[...], w_theirs[k][...], preferred_element_type=jnp.float32)
                out[k] = total.astype(jnp.bfloat16)


def out_project(place, mine, theirs, w_mine, w_theirs, shifts):
    rows = mine.shape[0]
    context = pl.BlockSpec((rows, FS), lambda i, p: (0, 0))
    first = shifts[0]
    weights = [
        pl.BlockSpec((FS, FS), lambda i, p, k=k: (0, 2 * (3 * k + lax.rem(p[1] + first + i, 3)) + p[0]))
        for k in range(FAR)
    ]
    return pl.pallas_call(
        out_kernel,
        grid_spec=pltpu.PrefetchScalarGridSpec(
            num_scalar_prefetch=1,
            grid=(len(shifts),),
            in_specs=[context, context] + weights + weights,
            out_specs=[pl.BlockSpec((FAR, rows, FS), lambda i, p: (0, 0, 0))] * len(shifts),
        ),
        out_shape=[jax.ShapeDtypeStruct((FAR, rows, FS), jnp.bfloat16)] * len(shifts),
        compiler_params=pltpu.CompilerParams(vmem_limit_bytes=VMEM),
        cost_estimate=pl.CostEstimate(
            flops=len(shifts) * 4 * rows * FS * FAR * FS,
            bytes_accessed=len(shifts) * 2 * FAR * FS * (rows + 2 * FS),
            transcendentals=0,
        ),
        name="out_project",
    )(place, mine, theirs, *[w_mine] * FAR, *[w_theirs] * FAR)


def sum_over_chips(place, context, theirs, w_mine, w_theirs, lengths, packing):
    up, down = out_project(place, context, theirs, w_mine, w_theirs, (1, 2))
    up, lengths, packing = lax.optimization_barrier((up, lengths, packing))
    picks = make_picks(place, lengths, packing, context.shape[0])
    below = lax.ppermute(up, "tensor", [(t, (t + 2) % NT) for t in range(NT)])
    above = lax.ppermute(down, "tensor", [(t, (t - 2) % NT) for t in range(NT)])
    (own,) = out_project(place, context, theirs, w_mine, w_theirs, (0,))
    three = own.astype(jnp.float32) + below.astype(jnp.float32) + above.astype(jnp.float32)
    three, *picks = lax.optimization_barrier((three.astype(jnp.bfloat16), *picks))
    parts = lax.all_to_all(
        three, "tensor", split_axis=0, concat_axis=0, tiled=True,
        axis_index_groups=FAR_GROUPS,
    )
    return jnp.sum(parts.astype(jnp.float32), axis=0), *picks


def split_kernel(x_ref, head, tail):
    head[...] = x_ref[:AG_ROWS]
    last = x_ref[AG_ROWS : AG_ROWS + tail.shape[1]]
    for t in range(NT):
        tail[t] = last


def gather_rows(rollout, rows):
    if rows == AG_ROWS:
        head, tail = rollout[:rows], None
    else:
        vm = pl.BlockSpec(memory_space=pltpu.VMEM)
        head, last = pl.pallas_call(
            split_kernel,
            in_specs=[vm],
            out_specs=[vm, vm],
            out_shape=[
                jax.ShapeDtypeStruct((AG_ROWS, FS), jnp.bfloat16),
                jax.ShapeDtypeStruct((NT, rows - AG_ROWS, FS), jnp.bfloat16),
            ],
            compiler_params=pltpu.CompilerParams(vmem_limit_bytes=VMEM),
            name="split_rows",
        )(rollout)
        tail = lax.all_to_all(last, "tensor", split_axis=0, concat_axis=0, tiled=True)
    return lax.all_gather(head, "tensor", axis=0, axis_index_groups=Z_GROUPS), tail


def along_lanes(row):
    first = lax.broadcasted_iota(jnp.int32, (RPS, RPS), 0)
    second = lax.broadcasted_iota(jnp.int32, (RPS, RPS), 1)
    column = jnp.sum(jnp.where(first == second, row, 0.0), axis=1, keepdims=True)
    return jnp.sum(jnp.where(first <= second, column, 0.0), axis=0, keepdims=True)


def picks_kernel(core, lengths, pack, out_pick, in_pick):
    here = core[3]
    slots = RPS * MAXLEN
    lane = lax.broadcasted_iota(jnp.int32, (RPS, RPS), 1)
    sub = lax.broadcasted_iota(jnp.int32, (RPS, RPS), 0)
    own = lengths[pl.ds(here, 1), :].astype(jnp.float32)
    start = along_lanes(own) - own
    packed = pack[...]
    which = jnp.sum(jnp.where(packed // RPS == here, (packed % RPS).astype(jnp.float32), 0.0), axis=1, keepdims=True)
    chosen = which == lane.astype(jnp.float32)
    o_start = jnp.sum(jnp.where(chosen, start, 0.0), axis=1, keepdims=True)
    o_len = jnp.sum(jnp.where(chosen, own, 0.0), axis=1, keepdims=True)
    wide = lax.broadcasted_iota(jnp.int32, (RPS, 128), 1)
    both = jnp.where(wide == 0, o_start, jnp.where(wide == 1, o_len, 0.0)).astype(jnp.bfloat16)
    owner_of = lax.broadcasted_iota(jnp.int32, (slots, RPS), 0) // MAXLEN
    spread = jnp.where(owner_of == lax.broadcasted_iota(jnp.int32, (slots, RPS), 1), 1.0, 0.0).astype(jnp.bfloat16)
    both = jnp.dot(spread, both, preferred_element_type=jnp.float32)
    slot = (lax.broadcasted_iota(jnp.int32, (slots, 1), 0) % MAXLEN).astype(jnp.float32)
    row = jnp.where(slot < both[:, 1:2], both[:, 0:1] + slot, -1.0)
    places = lax.broadcasted_iota(jnp.int32, out_pick.shape, 1).astype(jnp.float32)
    out_pick[...] = jnp.where(places == row, 1.0, 0.0).astype(jnp.bfloat16)
    mine = pack[pl.ds(here, 1), :]
    from_source = mine // RPS
    is_source = jnp.where(sub == from_source, 1.0, 0.0).astype(jnp.bfloat16)
    by_k = lax.dot_general(
        lengths[...].astype(jnp.float32).astype(jnp.bfloat16), is_source, (((0,), (0,)), ((), ())),
        preferred_element_type=jnp.float32,
    )
    length = jnp.sum(jnp.where(sub == mine % RPS, by_k, 0.0), axis=0, keepdims=True)
    end = along_lanes(length)
    begin = end - length
    place = lax.broadcasted_iota(jnp.int32, (slots, RPS), 0).astype(jnp.float32)
    inside = (place >= begin) & (place < end)
    at = jnp.where(inside, from_source.astype(jnp.float32) * MAXLEN + place - begin + 1.0, 0.0)
    at = jnp.sum(at, axis=1, keepdims=True) - 1.0
    arrived = lax.broadcasted_iota(jnp.int32, in_pick.shape, 1).astype(jnp.float32)
    in_pick[...] = jnp.where(arrived == at, 1.0, 0.0).astype(jnp.bfloat16)


def make_picks(core, lengths, packing, rows):
    vm = pl.BlockSpec(memory_space=pltpu.VMEM)
    return pl.pallas_call(
        picks_kernel,
        in_specs=[pl.BlockSpec(memory_space=pltpu.SMEM), vm, vm],
        out_specs=[vm, vm],
        out_shape=[
            jax.ShapeDtypeStruct((RPS * MAXLEN, rows), jnp.bfloat16),
            jax.ShapeDtypeStruct((RPS * MAXLEN, RPS * MAXLEN), jnp.bfloat16),
        ],
        compiler_params=pltpu.CompilerParams(vmem_limit_bytes=VMEM),
        name="make_picks",
    )(core, lengths, packing.reshape(RPS, RPS))


def layer(rows, rollout, lengths, packing, norm_gain, query_weight, keyval_weight, out_weight):
    source = lax.axis_index("dp")
    tensor_index = lax.axis_index("tensor")
    core = jnp.stack([tensor_index % 2, tensor_index // 2 % 3, tensor_index // 2 % 2, source]).astype(jnp.int32)
    x = rollout[:rows]

    mine, tail = gather_rows(rollout, rows)
    gain = norm_gain.reshape(NT, 1, FS)
    wk = keyval_weight.T
    mine, tail, wk_theirs = lax.optimization_barrier((mine, tail, swap(wk)))
    theirs = swap(mine)
    keyval, inverse = project_kv(core, mine, tail, gain, wk, wk_theirs)
    first = lax.ppermute(keyval, "tensor", kv_pairs(True))
    second = lax.ppermute(keyval, "tensor", kv_pairs(False))
    q, cosine, sine, bias = project_q(core, mine, theirs, tail, gain, query_weight, inverse, lengths)
    context = attend(core, q, first, second, cosine, sine, bias)
    summed, out_pick, in_pick = sum_over_chips(
        core, context, swap(context), out_weight, swap(out_weight), lengths, packing
    )
    result = (summed + x.astype(jnp.float32)).astype(jnp.bfloat16)
    outgoing = jnp.dot(out_pick, result, preferred_element_type=jnp.float32).astype(jnp.bfloat16)
    incoming = lax.all_to_all(
        outgoing.reshape(RPS, MAXLEN, FS), "dp", split_axis=0, concat_axis=0, tiled=True
    ).reshape(RPS * MAXLEN, FS)
    return jnp.dot(in_pick, incoming, preferred_element_type=jnp.float32).astype(jnp.bfloat16)


def body(rollout, lengths, packing, norm_gain, query_weight, keyval_weight, out_weight):
    longest = jnp.max(jnp.sum(lengths, axis=1))
    size = sum((longest > cap).astype(jnp.int32) for cap in CAPS[:-1])
    return lax.switch(
        size,
        [functools.partial(layer, cap) for cap in CAPS],
        rollout, lengths, packing, norm_gain, query_weight, keyval_weight, out_weight,
    )


def solution(mesh):
    in_specs = (
        P("dp", "tensor"),
        P(),
        P(),
        P(),
        P(None, "tensor"),
        P(None, "tensor"),
        P("tensor", None),
    )
    out_specs = P("dp", "tensor")
    return jax.shard_map(body, mesh=mesh, in_specs=in_specs, out_specs=out_specs, check_vma=False)
```

```python
import functools
import math

import jax
import jax.numpy as jnp
import numpy as np
from jax import lax
from jax.experimental import pallas as pl
from jax.experimental.pallas import tpu as pltpu
from jax.sharding import PartitionSpec as P

D = 6144
HD = 128
MAXLEN = 8
NZ = 12
NT = 24
FS = 256
RPS = 32
KVS = 64
EPS = 1e-05
ROPE_BASE = 500000.0
AG_ROWS = 168
VMEM = 12 * 1024 * 1024

Z_GROUPS = [[z * 2 + c for z in range(NZ)] for c in range(2)]
FAR = 4
FAR_GROUPS = [[(3 * k + r) * 2 + c for k in range(FAR)] for r in range(3) for c in range(2)]
SWAP = [(t, t ^ 1) for t in range(NT)]


STEPS = 3
PER = NZ // STEPS
CAPS = (168, 176, 192, 256)


def rope_tables():
    frequency = ROPE_BASE ** (-np.arange(HD // 2) * 2.0 / HD)
    angles = np.arange(MAXLEN)[:, None] * np.concatenate([frequency, frequency])[None, :]
    sign = np.where(np.arange(HD) < HD // 2, -1.0, 1.0)[None, :]
    return np.cos(angles).astype(np.float32), (np.sin(angles) * sign).astype(np.float32)


def turn(v, cosine, sine):
    turned = jnp.concatenate([v[:, HD // 2 :], v[:, : HD // 2]], axis=1)
    return (v * cosine + turned * sine).astype(jnp.bfloat16)


def documents(lengths, source, rows):
    own = lengths[pl.ds(source, 1), :].astype(jnp.float32)
    first = lax.broadcasted_iota(jnp.int32, (RPS, RPS), 0)
    second = lax.broadcasted_iota(jnp.int32, (RPS, RPS), 1)
    column = jnp.sum(jnp.where(first == second, own, 0.0), axis=1, keepdims=True)
    end = jnp.sum(jnp.where(first <= second, column, 0.0), axis=0, keepdims=True)
    end_column = jnp.sum(jnp.where(second <= first, own, 0.0), axis=1, keepdims=True)
    start = end - own
    place = lax.broadcasted_iota(jnp.int32, (rows, RPS), 0).astype(jnp.float32)
    doc = jnp.sum(jnp.where(place >= end, 1.0, 0.0), axis=1, keepdims=True)
    begun = jnp.max(jnp.where(start <= place, start, 0.0), axis=1, keepdims=True)
    position = jnp.where(doc < RPS, place[:, :1] - begun, 0.0)
    along = lax.broadcasted_iota(jnp.int32, (RPS, rows), 1).astype(jnp.float32)
    doc_row = jnp.sum(jnp.where(along >= end_column, 1.0, 0.0), axis=0, keepdims=True)
    return doc, position, doc_row


def kv_pairs(first):
    pairs = []
    for z in range(NZ):
        g, value = z % (NZ // 2), z // (NZ // 2)
        to = 2 * g + (value if first else 1 - value)
        pairs += [(2 * z + c, 2 * to + c) for c in range(2)]
    return pairs


def swap(v):
    return lax.ppermute(v, "tensor", SWAP)


def rows_of(refs, j, side):
    head, tail = refs
    x = head[j].astype(jnp.float32)
    if tail is not None:
        x = jnp.concatenate([x, tail[2 * j + side].astype(jnp.float32)], axis=0)
    return x


def kv_kernel(has_tail, core, mine, theirs, *rest):
    if has_tail:
        tail, *rest = rest
    else:
        tail = None
    gain, wk_m, wk_t, kv_out, inv_out, kv_acc, sq_acc = rest
    step = pl.program_id(0)
    c = core[0]

    @pl.when(step == 0)
    def _():
        kv_acc[...] = jnp.zeros_like(kv_acc)
        sq_acc[...] = jnp.zeros_like(sq_acc)

    total, squares = kv_acc[...], sq_acc[...]
    for j in range(PER):
        for x_ref, side in ((mine, c), (theirs, 1 - c)):
            x = rows_of((x_ref, tail), j, side)
            square = x * x
            squares += square[:, :128] + square[:, 128:]
            scaled = (x * gain[2 * j + side]).astype(jnp.bfloat16)
            at = pl.ds(pl.multiple_of((2 * j + side) * FS, FS), FS)
            w = jnp.concatenate([wk_m[:, at], wk_t[:, at]], axis=0)
            total += lax.dot_general(
                scaled, w, (((1,), (1,)), ((), ())), preferred_element_type=jnp.float32
            )
    kv_acc[...] = total
    sq_acc[...] = squares

    @pl.when(step == STEPS - 1)
    def _():
        inverse = lax.rsqrt(jnp.sum(squares, axis=1, keepdims=True) / D + EPS)
        out = total * inverse
        turned = jnp.concatenate([out[:, KVS:], out[:, :KVS]], axis=1)
        kv_out[...] = jnp.where(c == 0, out, turned).astype(jnp.bfloat16)
        inv_out[...] = jnp.broadcast_to(inverse, inv_out.shape)


def q_kernel(has_tail, core, mine, theirs, *rest):
    if has_tail:
        tail, *rest = rest
    else:
        tail = None
    gain, wq_m, wq_t, inv, lengths, cos_t, sin_t, q_out, cos_out, sin_out, bias_out, q_acc = rest
    step = pl.program_id(0)
    c = core[0]
    rows = q_acc.shape[0]

    @pl.when(step == 0)
    def _():
        q_acc[...] = jnp.zeros_like(q_acc)
        doc, position, doc_row = documents(lengths, core[3], rows)
        cosine = jnp.broadcast_to(cos_t[0:1], (rows, HD))
        sine = jnp.broadcast_to(sin_t[0:1], (rows, HD))
        for m in range(1, MAXLEN):
            here = jnp.broadcast_to(position == m, (rows, HD))
            cosine = jnp.where(here, cos_t[m : m + 1], cosine)
            sine = jnp.where(here, sin_t[m : m + 1], sine)
        cos_out[...] = cosine
        sin_out[...] = sine
        place_q = lax.broadcasted_iota(jnp.int32, (rows, rows), 0)
        place_k = lax.broadcasted_iota(jnp.int32, (rows, rows), 1)
        allowed = (doc == doc_row) & (place_k <= place_q)
        bias_out[...] = jnp.where(allowed, 0.0, -jnp.inf)

    total = q_acc[...]
    for j in range(PER):
        for x_ref, wq, side in ((mine, wq_m, c), (theirs, wq_t, 1 - c)):
            x = rows_of((x_ref, tail), j, side)
            scaled = (x * gain[2 * j + side]).astype(jnp.bfloat16)
            total += jnp.dot(scaled, wq[j, 0], preferred_element_type=jnp.float32)
    q_acc[...] = total

    @pl.when(step == STEPS - 1)
    def _():
        for h in range(2):
            head = total[:, h * HD : (h + 1) * HD] * inv[...]
            q_out[:, h * HD : (h + 1) * HD] = turn(head, cos_out[...], sin_out[...])


def x_specs(xs, tail):
    specs = [pl.BlockSpec((PER, x.shape[1], FS), lambda i, c: (i, 0, 0)) for x in xs]
    if tail is not None:
        specs.append(pl.BlockSpec((2 * PER, tail.shape[1], FS), lambda i, c: (i, 0, 0)))
    specs.append(pl.BlockSpec((2 * PER, 1, FS), lambda i, c: (i, 0, 0)))
    return specs


def project_kv(core, mine, theirs, tail, gain, wk_m, wk_t):
    rows = mine.shape[1] + (0 if tail is None else tail.shape[1])
    whole = pl.BlockSpec((rows, HD), lambda i, c: (0, 0))
    wk_spec = pl.BlockSpec((KVS, 2 * PER * FS), lambda i, c: (0, i))
    return pl.pallas_call(
        functools.partial(kv_kernel, tail is not None),
        grid_spec=pltpu.PrefetchScalarGridSpec(
            num_scalar_prefetch=1,
            grid=(STEPS,),
            in_specs=x_specs([mine, theirs], tail) + [wk_spec, wk_spec],
            out_specs=[whole, whole],
            scratch_shapes=[pltpu.VMEM((rows, HD), jnp.float32), pltpu.VMEM((rows, HD), jnp.float32)],
        ),
        out_shape=[
            jax.ShapeDtypeStruct((rows, HD), jnp.bfloat16),
            jax.ShapeDtypeStruct((rows, HD), jnp.float32),
        ],
        compiler_params=pltpu.CompilerParams(vmem_limit_bytes=VMEM),
        cost_estimate=pl.CostEstimate(
            flops=2 * rows * D * HD, bytes_accessed=2 * D * (rows + HD), transcendentals=rows
        ),
        name="project_kv",
    )(core, mine, theirs, *([] if tail is None else [tail]), gain, wk_m, wk_t)


def project_q(core, mine, theirs, tail, gain, wq, inverse, lengths):
    rows = inverse.shape[0]
    wq4 = wq.reshape(NZ, 2, FS, FS)
    whole = lambda i, c: (0, 0)
    cos_t, sin_t = rope_tables()
    return pl.pallas_call(
        functools.partial(q_kernel, tail is not None),
        grid_spec=pltpu.PrefetchScalarGridSpec(
            num_scalar_prefetch=1,
            grid=(STEPS,),
            in_specs=x_specs([mine, theirs], tail)
            + [
                pl.BlockSpec((PER, 1, FS, FS), lambda i, c: (i, c[0], 0, 0)),
                pl.BlockSpec((PER, 1, FS, FS), lambda i, c: (i, 1 - c[0], 0, 0)),
                pl.BlockSpec((rows, HD), whole),
                pl.BlockSpec((RPS, RPS), whole),
                pl.BlockSpec((MAXLEN, HD), whole),
                pl.BlockSpec((MAXLEN, HD), whole),
            ],
            out_specs=[
                pl.BlockSpec((rows, FS), whole),
                pl.BlockSpec((rows, HD), whole),
                pl.BlockSpec((rows, HD), whole),
                pl.BlockSpec((rows, rows), whole),
            ],
            scratch_shapes=[pltpu.VMEM((rows, FS), jnp.float32)],
        ),
        out_shape=[
            jax.ShapeDtypeStruct((rows, FS), jnp.bfloat16),
            jax.ShapeDtypeStruct((rows, HD), jnp.float32),
            jax.ShapeDtypeStruct((rows, HD), jnp.float32),
            jax.ShapeDtypeStruct((rows, rows), jnp.float32),
        ],
        compiler_params=pltpu.CompilerParams(vmem_limit_bytes=VMEM),
        cost_estimate=pl.CostEstimate(
            flops=2 * rows * D * FS, bytes_accessed=2 * D * (rows + FS), transcendentals=0
        ),
        name="project_q",
    )(core, mine, theirs, *([] if tail is None else [tail]), gain, wq4, wq4, inverse,
      lengths, cos_t, sin_t)


def attention_kernel(core, q_ref, first, second, cos_ref, sin_ref, bias_ref, out_ref):
    one, two = first[...].astype(jnp.float32), second[...].astype(jnp.float32)
    swapped = core[2] == 1
    keys = jnp.where(swapped, two, one)
    values = jnp.where(swapped, one, two).astype(jnp.bfloat16)
    k_rot = turn(keys, cos_ref[...], sin_ref[...])
    for h in range(2):
        scores = lax.dot_general(
            q_ref[:, h * HD : (h + 1) * HD], k_rot, (((1,), (1,)), ((), ())), preferred_element_type=jnp.float32
        )
        masked = scores * (1 / math.sqrt(HD)) + bias_ref[...]
        exponent = jnp.exp(masked - jnp.max(masked, axis=1, keepdims=True))
        weights = (exponent / jnp.sum(exponent, axis=1, keepdims=True)).astype(jnp.bfloat16)
        context = jnp.dot(weights, values, preferred_element_type=jnp.float32)
        out_ref[:, h * HD : (h + 1) * HD] = context.astype(jnp.bfloat16)


def attend(core, q, first, second, cosine, sine, bias):
    rows = q.shape[0]
    vm = pl.BlockSpec(memory_space=pltpu.VMEM)
    return pl.pallas_call(
        attention_kernel,
        in_specs=[pl.BlockSpec(memory_space=pltpu.SMEM)] + [vm] * 6,
        out_specs=vm,
        out_shape=jax.ShapeDtypeStruct((rows, FS), jnp.bfloat16),
        compiler_params=pltpu.CompilerParams(vmem_limit_bytes=VMEM),
        cost_estimate=pl.CostEstimate(
            flops=8 * rows * rows * HD, bytes_accessed=4 * rows * FS, transcendentals=2 * rows * rows
        ),
        name="attend",
    )(core, q, first, second, cosine, sine, bias)


def out_kernel(place, mine, theirs, *rest):
    w_mine, w_theirs, outs = rest[:FAR], rest[FAR : 2 * FAR], rest[2 * FAR :]
    for at, out in enumerate(outs):

        @pl.when(pl.program_id(0) == at)
        def _():
            for k in range(FAR):
                total = jnp.dot(mine[...], w_mine[k][...], preferred_element_type=jnp.float32)
                total += jnp.dot(theirs[...], w_theirs[k][...], preferred_element_type=jnp.float32)
                out[k] = total.astype(jnp.bfloat16)


def out_project(place, mine, theirs, w_mine, w_theirs, shifts):
    rows = mine.shape[0]
    context = pl.BlockSpec((rows, FS), lambda i, p: (0, 0))
    first = shifts[0]
    weights = [
        pl.BlockSpec((FS, FS), lambda i, p, k=k: (0, 2 * (3 * k + lax.rem(p[1] + first + i, 3)) + p[0]))
        for k in range(FAR)
    ]
    return pl.pallas_call(
        out_kernel,
        grid_spec=pltpu.PrefetchScalarGridSpec(
            num_scalar_prefetch=1,
            grid=(len(shifts),),
            in_specs=[context, context] + weights + weights,
            out_specs=[pl.BlockSpec((FAR, rows, FS), lambda i, p: (0, 0, 0))] * len(shifts),
        ),
        out_shape=[jax.ShapeDtypeStruct((FAR, rows, FS), jnp.bfloat16)] * len(shifts),
        compiler_params=pltpu.CompilerParams(vmem_limit_bytes=VMEM),
        cost_estimate=pl.CostEstimate(
            flops=len(shifts) * 4 * rows * FS * FAR * FS,
            bytes_accessed=len(shifts) * 2 * FAR * FS * (rows + 2 * FS),
            transcendentals=0,
        ),
        name="out_project",
    )(place, mine, theirs, *[w_mine] * FAR, *[w_theirs] * FAR)


def sum_over_chips(place, context, theirs, w_mine, w_theirs, lengths, packing):
    up, down = out_project(place, context, theirs, w_mine, w_theirs, (1, 2))
    up, lengths, packing = lax.optimization_barrier((up, lengths, packing))
    picks = make_picks(place, lengths, packing, context.shape[0])
    below = lax.ppermute(up, "tensor", [(t, (t + 2) % NT) for t in range(NT)])
    above = lax.ppermute(down, "tensor", [(t, (t - 2) % NT) for t in range(NT)])
    (own,) = out_project(place, context, theirs, w_mine, w_theirs, (0,))
    three = own.astype(jnp.float32) + below.astype(jnp.float32) + above.astype(jnp.float32)
    three, *picks = lax.optimization_barrier((three.astype(jnp.bfloat16), *picks))
    parts = lax.all_to_all(
        three, "tensor", split_axis=0, concat_axis=0, tiled=True,
        axis_index_groups=FAR_GROUPS,
    )
    return jnp.sum(parts.astype(jnp.float32), axis=0), *picks


def split_kernel(x_ref, head, tail):
    head[...] = x_ref[:AG_ROWS]
    last = x_ref[AG_ROWS : AG_ROWS + tail.shape[1]]
    for t in range(NT):
        tail[t] = last


def gather_rows(rollout, rows):
    if rows == AG_ROWS:
        head, tail = rollout[:rows], None
    else:
        vm = pl.BlockSpec(memory_space=pltpu.VMEM)
        head, last = pl.pallas_call(
            split_kernel,
            in_specs=[vm],
            out_specs=[vm, vm],
            out_shape=[
                jax.ShapeDtypeStruct((AG_ROWS, FS), jnp.bfloat16),
                jax.ShapeDtypeStruct((NT, rows - AG_ROWS, FS), jnp.bfloat16),
            ],
            compiler_params=pltpu.CompilerParams(vmem_limit_bytes=VMEM),
            name="split_rows",
        )(rollout)
        tail = lax.all_to_all(last, "tensor", split_axis=0, concat_axis=0, tiled=True)
    return lax.all_gather(head, "tensor", axis=0, axis_index_groups=Z_GROUPS), tail


def along_lanes(row):
    first = lax.broadcasted_iota(jnp.int32, (RPS, RPS), 0)
    second = lax.broadcasted_iota(jnp.int32, (RPS, RPS), 1)
    column = jnp.sum(jnp.where(first == second, row, 0.0), axis=1, keepdims=True)
    return jnp.sum(jnp.where(first <= second, column, 0.0), axis=0, keepdims=True)


def picks_kernel(core, lengths, pack, out_pick, in_pick):
    here = core[3]
    slots = RPS * MAXLEN
    lane = lax.broadcasted_iota(jnp.int32, (RPS, RPS), 1)
    sub = lax.broadcasted_iota(jnp.int32, (RPS, RPS), 0)
    own = lengths[pl.ds(here, 1), :].astype(jnp.float32)
    start = along_lanes(own) - own
    packed = pack[...]
    which = jnp.sum(jnp.where(packed // RPS == here, (packed % RPS).astype(jnp.float32), 0.0), axis=1, keepdims=True)
    chosen = which == lane.astype(jnp.float32)
    o_start = jnp.sum(jnp.where(chosen, start, 0.0), axis=1, keepdims=True)
    o_len = jnp.sum(jnp.where(chosen, own, 0.0), axis=1, keepdims=True)
    wide = lax.broadcasted_iota(jnp.int32, (RPS, 128), 1)
    both = jnp.where(wide == 0, o_start, jnp.where(wide == 1, o_len, 0.0)).astype(jnp.bfloat16)
    owner_of = lax.broadcasted_iota(jnp.int32, (slots, RPS), 0) // MAXLEN
    spread = jnp.where(owner_of == lax.broadcasted_iota(jnp.int32, (slots, RPS), 1), 1.0, 0.0).astype(jnp.bfloat16)
    both = jnp.dot(spread, both, preferred_element_type=jnp.float32)
    slot = (lax.broadcasted_iota(jnp.int32, (slots, 1), 0) % MAXLEN).astype(jnp.float32)
    row = jnp.where(slot < both[:, 1:2], both[:, 0:1] + slot, -1.0)
    places = lax.broadcasted_iota(jnp.int32, out_pick.shape, 1).astype(jnp.float32)
    out_pick[...] = jnp.where(places == row, 1.0, 0.0).astype(jnp.bfloat16)
    mine = pack[pl.ds(here, 1), :]
    from_source = mine // RPS
    is_source = jnp.where(sub == from_source, 1.0, 0.0).astype(jnp.bfloat16)
    by_k = lax.dot_general(
        lengths[...].astype(jnp.float32).astype(jnp.bfloat16), is_source, (((0,), (0,)), ((), ())),
        preferred_element_type=jnp.float32,
    )
    length = jnp.sum(jnp.where(sub == mine % RPS, by_k, 0.0), axis=0, keepdims=True)
    end = along_lanes(length)
    begin = end - length
    place = lax.broadcasted_iota(jnp.int32, (slots, RPS), 0).astype(jnp.float32)
    inside = (place >= begin) & (place < end)
    at = jnp.where(inside, from_source.astype(jnp.float32) * MAXLEN + place - begin + 1.0, 0.0)
    at = jnp.sum(at, axis=1, keepdims=True) - 1.0
    arrived = lax.broadcasted_iota(jnp.int32, in_pick.shape, 1).astype(jnp.float32)
    in_pick[...] = jnp.where(arrived == at, 1.0, 0.0).astype(jnp.bfloat16)


def make_picks(core, lengths, packing, rows):
    vm = pl.BlockSpec(memory_space=pltpu.VMEM)
    return pl.pallas_call(
        picks_kernel,
        in_specs=[pl.BlockSpec(memory_space=pltpu.SMEM), vm, vm],
        out_specs=[vm, vm],
        out_shape=[
            jax.ShapeDtypeStruct((RPS * MAXLEN, rows), jnp.bfloat16),
            jax.ShapeDtypeStruct((RPS * MAXLEN, RPS * MAXLEN), jnp.bfloat16),
        ],
        compiler_params=pltpu.CompilerParams(vmem_limit_bytes=VMEM),
        name="make_picks",
    )(core, lengths, packing.reshape(RPS, RPS))


def layer(rows, rollout, lengths, packing, norm_gain, query_weight, keyval_weight, out_weight):
    source = lax.axis_index("dp")
    tensor_index = lax.axis_index("tensor")
    core = jnp.stack([tensor_index % 2, tensor_index // 2 % 3, tensor_index // 2 % 2, source]).astype(jnp.int32)
    x = rollout[:rows]

    mine, tail = gather_rows(rollout, rows)
    gain = norm_gain.reshape(NT, 1, FS)
    wk = keyval_weight.T
    mine, tail, wk = lax.optimization_barrier((mine, tail, wk))
    theirs = swap(mine)
    keyval, inverse = project_kv(core, mine, theirs, tail, gain, wk, swap(wk))
    first = lax.ppermute(keyval, "tensor", kv_pairs(True))
    second = lax.ppermute(keyval, "tensor", kv_pairs(False))
    q, cosine, sine, bias = project_q(core, mine, theirs, tail, gain, query_weight, inverse, lengths)
    context = attend(core, q, first, second, cosine, sine, bias)
    summed, out_pick, in_pick = sum_over_chips(
        core, context, swap(context), out_weight, swap(out_weight), lengths, packing
    )
    result = (summed + x.astype(jnp.float32)).astype(jnp.bfloat16)
    outgoing = jnp.dot(out_pick, result, preferred_element_type=jnp.float32).astype(jnp.bfloat16)
    incoming = lax.all_to_all(
        outgoing.reshape(RPS, MAXLEN, FS), "dp", split_axis=0, concat_axis=0, tiled=True
    ).reshape(RPS * MAXLEN, FS)
    return jnp.dot(in_pick, incoming, preferred_element_type=jnp.float32).astype(jnp.bfloat16)


def size_kernel(lengths, size):
    longest = jnp.max(jnp.sum(lengths[...].astype(jnp.float32), axis=1, keepdims=True))
    at = jnp.int32(0)
    for cap in CAPS[:-1]:
        at += (longest > cap).astype(jnp.int32)
    size[0] = at


def body(rollout, lengths, packing, norm_gain, query_weight, keyval_weight, out_weight):
    size = pl.pallas_call(
        size_kernel,
        in_specs=[pl.BlockSpec(memory_space=pltpu.VMEM)],
        out_specs=pl.BlockSpec(memory_space=pltpu.SMEM),
        out_shape=jax.ShapeDtypeStruct((1,), jnp.int32),
        compiler_params=pltpu.CompilerParams(vmem_limit_bytes=VMEM),
        name="size",
    )(lengths)
    return lax.switch(
        size[0],
        [functools.partial(layer, cap) for cap in CAPS],
        rollout, lengths, packing, norm_gain, query_weight, keyval_weight, out_weight,
    )


def solution(mesh):
    in_specs = (
        P("dp", "tensor"),
        P(),
        P(),
        P(),
        P(None, "tensor"),
        P(None, "tensor"),
        P("tensor", None),
    )
    out_specs = P("dp", "tensor")
    return jax.shard_map(body, mesh=mesh, in_specs=in_specs, out_specs=out_specs, check_vma=False)
```

```python
import functools
import math

import jax
import jax.numpy as jnp
import numpy as np
from jax import lax
from jax.experimental import pallas as pl
from jax.experimental.pallas import tpu as pltpu
from jax.sharding import PartitionSpec as P

D = 6144
HD = 128
MAXLEN = 8
NZ = 12
NT = 24
FS = 256
RPS = 32
KVS = 64
EPS = 1e-05
ROPE_BASE = 500000.0
AG_ROWS = 168
VMEM = 12 * 1024 * 1024

Z_GROUPS = [[z * 2 + c for z in range(NZ)] for c in range(2)]
FAR = 4
FAR_GROUPS = [[(3 * k + r) * 2 + c for k in range(FAR)] for r in range(3) for c in range(2)]
SWAP = [(t, t ^ 1) for t in range(NT)]


STEPS = 3
PER = NZ // STEPS
CAPS = (168, 176, 192, 256)


def rope_tables():
    frequency = ROPE_BASE ** (-np.arange(HD // 2) * 2.0 / HD)
    angles = np.arange(MAXLEN)[:, None] * np.concatenate([frequency, frequency])[None, :]
    sign = np.where(np.arange(HD) < HD // 2, -1.0, 1.0)[None, :]
    return np.cos(angles).astype(np.float32), (np.sin(angles) * sign).astype(np.float32)


def turn(v, cosine, sine):
    turned = jnp.concatenate([v[:, HD // 2 :], v[:, : HD // 2]], axis=1)
    return (v * cosine + turned * sine).astype(jnp.bfloat16)


def documents(lengths, source, rows):
    own = lengths[pl.ds(source, 1), :].astype(jnp.float32)
    first = lax.broadcasted_iota(jnp.int32, (RPS, RPS), 0)
    second = lax.broadcasted_iota(jnp.int32, (RPS, RPS), 1)
    column = jnp.sum(jnp.where(first == second, own, 0.0), axis=1, keepdims=True)
    end = jnp.sum(jnp.where(first <= second, column, 0.0), axis=0, keepdims=True)
    end_column = jnp.sum(jnp.where(second <= first, own, 0.0), axis=1, keepdims=True)
    start = end - own
    place = lax.broadcasted_iota(jnp.int32, (rows, RPS), 0).astype(jnp.float32)
    doc = jnp.sum(jnp.where(place >= end, 1.0, 0.0), axis=1, keepdims=True)
    begun = jnp.max(jnp.where(start <= place, start, 0.0), axis=1, keepdims=True)
    position = jnp.where(doc < RPS, place[:, :1] - begun, 0.0)
    along = lax.broadcasted_iota(jnp.int32, (RPS, rows), 1).astype(jnp.float32)
    doc_row = jnp.sum(jnp.where(along >= end_column, 1.0, 0.0), axis=0, keepdims=True)
    return doc, position, doc_row


def kv_pairs(first):
    pairs = []
    for z in range(NZ):
        g, value = z % (NZ // 2), z // (NZ // 2)
        to = 2 * g + (value if first else 1 - value)
        pairs += [(2 * z + c, 2 * to + c) for c in range(2)]
    return pairs


def swap(v):
    return lax.ppermute(v, "tensor", SWAP)


def rows_of(refs, j, side):
    head, tail = refs
    x = head[j].astype(jnp.float32)
    if tail is not None:
        x = jnp.concatenate([x, tail[2 * j + side].astype(jnp.float32)], axis=0)
    return x


def kv_kernel(has_tail, core, mine, theirs, *rest):
    if has_tail:
        tail, *rest = rest
    else:
        tail = None
    gain, wk_m, wk_t, kv_out, inv_out, kv_acc, sq_acc = rest
    step = pl.program_id(0)
    c = core[0]

    @pl.when(step == 0)
    def _():
        kv_acc[...] = jnp.zeros_like(kv_acc)
        sq_acc[...] = jnp.zeros_like(sq_acc)

    total, squares = kv_acc[...], sq_acc[...]
    for j in range(PER):
        for x_ref, side in ((mine, c), (theirs, 1 - c)):
            x = rows_of((x_ref, tail), j, side)
            square = x * x
            squares += square[:, :128] + square[:, 128:]
            scaled = (x * gain[2 * j + side]).astype(jnp.bfloat16)
            at = pl.ds(pl.multiple_of((2 * j + side) * FS, FS), FS)
            w = jnp.concatenate([wk_m[:, at], wk_t[:, at]], axis=0)
            total += lax.dot_general(
                scaled, w, (((1,), (1,)), ((), ())), preferred_element_type=jnp.float32
            )
    kv_acc[...] = total
    sq_acc[...] = squares

    @pl.when(step == STEPS - 1)
    def _():
        inverse = lax.rsqrt(jnp.sum(squares, axis=1, keepdims=True) / D + EPS)
        out = total * inverse
        turned = jnp.concatenate([out[:, KVS:], out[:, :KVS]], axis=1)
        kv_out[...] = jnp.where(c == 0, out, turned).astype(jnp.bfloat16)
        inv_out[...] = jnp.broadcast_to(inverse, inv_out.shape)


def q_kernel(has_tail, core, mine, theirs, *rest):
    if has_tail:
        tail, *rest = rest
    else:
        tail = None
    gain, wq_m, wq_t, inv, lengths, cos_t, sin_t, q_out, cos_out, sin_out, bias_out, q_acc = rest
    step = pl.program_id(0)
    c = core[0]
    rows = q_acc.shape[0]

    @pl.when(step == 0)
    def _():
        q_acc[...] = jnp.zeros_like(q_acc)
        doc, position, doc_row = documents(lengths, core[3], rows)
        cosine = jnp.broadcast_to(cos_t[0:1], (rows, HD))
        sine = jnp.broadcast_to(sin_t[0:1], (rows, HD))
        for m in range(1, MAXLEN):
            here = jnp.broadcast_to(position == m, (rows, HD))
            cosine = jnp.where(here, cos_t[m : m + 1], cosine)
            sine = jnp.where(here, sin_t[m : m + 1], sine)
        cos_out[...] = cosine
        sin_out[...] = sine
        place_q = lax.broadcasted_iota(jnp.int32, (rows, rows), 0)
        place_k = lax.broadcasted_iota(jnp.int32, (rows, rows), 1)
        allowed = (doc == doc_row) & (place_k <= place_q)
        bias_out[...] = jnp.where(allowed, 0.0, -jnp.inf)

    total = q_acc[...]
    for j in range(PER):
        for x_ref, wq, side in ((mine, wq_m, c), (theirs, wq_t, 1 - c)):
            x = rows_of((x_ref, tail), j, side)
            scaled = (x * gain[2 * j + side]).astype(jnp.bfloat16)
            total += jnp.dot(scaled, wq[j, 0], preferred_element_type=jnp.float32)
    q_acc[...] = total

    @pl.when(step == STEPS - 1)
    def _():
        for h in range(2):
            head = total[:, h * HD : (h + 1) * HD] * inv[...]
            q_out[:, h * HD : (h + 1) * HD] = turn(head, cos_out[...], sin_out[...])


def x_specs(xs, tail):
    specs = [pl.BlockSpec((PER, x.shape[1], FS), lambda i, c: (i, 0, 0)) for x in xs]
    if tail is not None:
        specs.append(pl.BlockSpec((2 * PER, tail.shape[1], FS), lambda i, c: (i, 0, 0)))
    specs.append(pl.BlockSpec((2 * PER, 1, FS), lambda i, c: (i, 0, 0)))
    return specs


def project_kv(core, mine, theirs, tail, gain, wk_m, wk_t):
    rows = mine.shape[1] + (0 if tail is None else tail.shape[1])
    whole = pl.BlockSpec((rows, HD), lambda i, c: (0, 0))
    wk_spec = pl.BlockSpec((KVS, 2 * PER * FS), lambda i, c: (0, i))
    return pl.pallas_call(
        functools.partial(kv_kernel, tail is not None),
        grid_spec=pltpu.PrefetchScalarGridSpec(
            num_scalar_prefetch=1,
            grid=(STEPS,),
            in_specs=x_specs([mine, theirs], tail) + [wk_spec, wk_spec],
            out_specs=[whole, whole],
            scratch_shapes=[pltpu.VMEM((rows, HD), jnp.float32), pltpu.VMEM((rows, HD), jnp.float32)],
        ),
        out_shape=[
            jax.ShapeDtypeStruct((rows, HD), jnp.bfloat16),
            jax.ShapeDtypeStruct((rows, HD), jnp.float32),
        ],
        compiler_params=pltpu.CompilerParams(vmem_limit_bytes=VMEM),
        cost_estimate=pl.CostEstimate(
            flops=2 * rows * D * HD, bytes_accessed=2 * D * (rows + HD), transcendentals=rows
        ),
        name="project_kv",
    )(core, mine, theirs, *([] if tail is None else [tail]), gain, wk_m, wk_t)


def project_q(core, mine, theirs, tail, gain, wq, inverse, lengths):
    rows = inverse.shape[0]
    wq4 = wq.reshape(NZ, 2, FS, FS)
    whole = lambda i, c: (0, 0)
    cos_t, sin_t = rope_tables()
    return pl.pallas_call(
        functools.partial(q_kernel, tail is not None),
        grid_spec=pltpu.PrefetchScalarGridSpec(
            num_scalar_prefetch=1,
            grid=(STEPS,),
            in_specs=x_specs([mine, theirs], tail)
            + [
                pl.BlockSpec((PER, 1, FS, FS), lambda i, c: (i, c[0], 0, 0)),
                pl.BlockSpec((PER, 1, FS, FS), lambda i, c: (i, 1 - c[0], 0, 0)),
                pl.BlockSpec((rows, HD), whole),
                pl.BlockSpec((RPS, RPS), whole),
                pl.BlockSpec((MAXLEN, HD), whole),
                pl.BlockSpec((MAXLEN, HD), whole),
            ],
            out_specs=[
                pl.BlockSpec((rows, FS), whole),
                pl.BlockSpec((rows, HD), whole),
                pl.BlockSpec((rows, HD), whole),
                pl.BlockSpec((rows, rows), whole),
            ],
            scratch_shapes=[pltpu.VMEM((rows, FS), jnp.float32)],
        ),
        out_shape=[
            jax.ShapeDtypeStruct((rows, FS), jnp.bfloat16),
            jax.ShapeDtypeStruct((rows, HD), jnp.float32),
            jax.ShapeDtypeStruct((rows, HD), jnp.float32),
            jax.ShapeDtypeStruct((rows, rows), jnp.float32),
        ],
        compiler_params=pltpu.CompilerParams(vmem_limit_bytes=VMEM),
        cost_estimate=pl.CostEstimate(
            flops=2 * rows * D * FS, bytes_accessed=2 * D * (rows + FS), transcendentals=0
        ),
        name="project_q",
    )(core, mine, theirs, *([] if tail is None else [tail]), gain, wq4, wq4, inverse,
      lengths, cos_t, sin_t)


def attention_kernel(core, q_ref, first, second, cos_ref, sin_ref, bias_ref, out_ref):
    one, two = first[...].astype(jnp.float32), second[...].astype(jnp.float32)
    swapped = core[2] == 1
    keys = jnp.where(swapped, two, one)
    values = jnp.where(swapped, one, two).astype(jnp.bfloat16)
    k_rot = turn(keys, cos_ref[...], sin_ref[...])
    for h in range(2):
        scores = lax.dot_general(
            q_ref[:, h * HD : (h + 1) * HD], k_rot, (((1,), (1,)), ((), ())), preferred_element_type=jnp.float32
        )
        masked = scores * (1 / math.sqrt(HD)) + bias_ref[...]
        exponent = jnp.exp(masked - jnp.max(masked, axis=1, keepdims=True))
        weights = (exponent / jnp.sum(exponent, axis=1, keepdims=True)).astype(jnp.bfloat16)
        context = jnp.dot(weights, values, preferred_element_type=jnp.float32)
        out_ref[:, h * HD : (h + 1) * HD] = context.astype(jnp.bfloat16)


def attend(core, q, first, second, cosine, sine, bias):
    rows = q.shape[0]
    vm = pl.BlockSpec(memory_space=pltpu.VMEM)
    return pl.pallas_call(
        attention_kernel,
        in_specs=[pl.BlockSpec(memory_space=pltpu.SMEM)] + [vm] * 6,
        out_specs=vm,
        out_shape=jax.ShapeDtypeStruct((rows, FS), jnp.bfloat16),
        compiler_params=pltpu.CompilerParams(vmem_limit_bytes=VMEM),
        cost_estimate=pl.CostEstimate(
            flops=8 * rows * rows * HD, bytes_accessed=4 * rows * FS, transcendentals=2 * rows * rows
        ),
        name="attend",
    )(core, q, first, second, cosine, sine, bias)


def out_kernel(place, mine, theirs, *rest):
    w_mine, w_theirs, outs = rest[:FAR], rest[FAR : 2 * FAR], rest[2 * FAR :]
    for at, out in enumerate(outs):

        @pl.when(pl.program_id(0) == at)
        def _():
            for k in range(FAR):
                total = jnp.dot(mine[...], w_mine[k][...], preferred_element_type=jnp.float32)
                total += jnp.dot(theirs[...], w_theirs[k][...], preferred_element_type=jnp.float32)
                out[k] = total.astype(jnp.bfloat16)


def out_project(place, mine, theirs, w_mine, w_theirs, shifts):
    rows = mine.shape[0]
    context = pl.BlockSpec((rows, FS), lambda i, p: (0, 0))
    turn_round = (lambda i, p: 1 + i + p[0] * (1 - 2 * i)) if len(shifts) == 2 else (lambda i, p: 0)
    weights = [
        pl.BlockSpec((FS, FS), lambda i, p, k=k: (0, 2 * (3 * k + lax.rem(p[1] + turn_round(i, p), 3)) + p[0]))
        for k in range(FAR)
    ]
    return pl.pallas_call(
        out_kernel,
        grid_spec=pltpu.PrefetchScalarGridSpec(
            num_scalar_prefetch=1,
            grid=(len(shifts),),
            in_specs=[context, context] + weights + weights,
            out_specs=[pl.BlockSpec((FAR, rows, FS), lambda i, p: (0, 0, 0))] * len(shifts),
        ),
        out_shape=[jax.ShapeDtypeStruct((FAR, rows, FS), jnp.bfloat16)] * len(shifts),
        compiler_params=pltpu.CompilerParams(vmem_limit_bytes=VMEM),
        cost_estimate=pl.CostEstimate(
            flops=len(shifts) * 4 * rows * FS * FAR * FS,
            bytes_accessed=len(shifts) * 2 * FAR * FS * (rows + 2 * FS),
            transcendentals=0,
        ),
        name="out_project",
    )(place, mine, theirs, *[w_mine] * FAR, *[w_theirs] * FAR)


def sum_over_chips(place, context, theirs, w_mine, w_theirs, lengths, packing):
    one, two = out_project(place, context, theirs, w_mine, w_theirs, (1, 2))
    one, lengths, packing = lax.optimization_barrier((one, lengths, packing))
    picks = make_picks(place, lengths, packing, context.shape[0])
    below = lax.ppermute(one, "tensor", [(t, (t + 2 - 4 * (t % 2)) % NT) for t in range(NT)])
    above = lax.ppermute(two, "tensor", [(t, (t - 2 + 4 * (t % 2)) % NT) for t in range(NT)])
    (own,) = out_project(place, context, theirs, w_mine, w_theirs, (0,))
    three = own.astype(jnp.float32) + below.astype(jnp.float32) + above.astype(jnp.float32)
    three, *picks = lax.optimization_barrier((three.astype(jnp.bfloat16), *picks))
    parts = lax.all_to_all(
        three, "tensor", split_axis=0, concat_axis=0, tiled=True,
        axis_index_groups=FAR_GROUPS,
    )
    return jnp.sum(parts.astype(jnp.float32), axis=0), *picks


def split_kernel(x_ref, head, tail):
    head[...] = x_ref[:AG_ROWS]
    last = x_ref[AG_ROWS : AG_ROWS + tail.shape[1]]
    for t in range(NT):
        tail[t] = last


def gather_rows(rollout, rows):
    if rows == AG_ROWS:
        head, tail = rollout[:rows], None
    else:
        vm = pl.BlockSpec(memory_space=pltpu.VMEM)
        head, last = pl.pallas_call(
            split_kernel,
            in_specs=[vm],
            out_specs=[vm, vm],
            out_shape=[
                jax.ShapeDtypeStruct((AG_ROWS, FS), jnp.bfloat16),
                jax.ShapeDtypeStruct((NT, rows - AG_ROWS, FS), jnp.bfloat16),
            ],
            compiler_params=pltpu.CompilerParams(vmem_limit_bytes=VMEM),
            name="split_rows",
        )(rollout)
        tail = lax.all_to_all(last, "tensor", split_axis=0, concat_axis=0, tiled=True)
    return lax.all_gather(head, "tensor", axis=0, axis_index_groups=Z_GROUPS), tail


def along_lanes(row):
    first = lax.broadcasted_iota(jnp.int32, (RPS, RPS), 0)
    second = lax.broadcasted_iota(jnp.int32, (RPS, RPS), 1)
    column = jnp.sum(jnp.where(first == second, row, 0.0), axis=1, keepdims=True)
    return jnp.sum(jnp.where(first <= second, column, 0.0), axis=0, keepdims=True)


def picks_kernel(core, lengths, pack, out_pick, in_pick):
    here = core[3]
    slots = RPS * MAXLEN
    lane = lax.broadcasted_iota(jnp.int32, (RPS, RPS), 1)
    sub = lax.broadcasted_iota(jnp.int32, (RPS, RPS), 0)
    own = lengths[pl.ds(here, 1), :].astype(jnp.float32)
    start = along_lanes(own) - own
    packed = pack[...]
    which = jnp.sum(jnp.where(packed // RPS == here, (packed % RPS).astype(jnp.float32), 0.0), axis=1, keepdims=True)
    chosen = which == lane.astype(jnp.float32)
    o_start = jnp.sum(jnp.where(chosen, start, 0.0), axis=1, keepdims=True)
    o_len = jnp.sum(jnp.where(chosen, own, 0.0), axis=1, keepdims=True)
    wide = lax.broadcasted_iota(jnp.int32, (RPS, 128), 1)
    both = jnp.where(wide == 0, o_start, jnp.where(wide == 1, o_len, 0.0)).astype(jnp.bfloat16)
    owner_of = lax.broadcasted_iota(jnp.int32, (slots, RPS), 0) // MAXLEN
    spread = jnp.where(owner_of == lax.broadcasted_iota(jnp.int32, (slots, RPS), 1), 1.0, 0.0).astype(jnp.bfloat16)
    both = jnp.dot(spread, both, preferred_element_type=jnp.float32)
    slot = (lax.broadcasted_iota(jnp.int32, (slots, 1), 0) % MAXLEN).astype(jnp.float32)
    row = jnp.where(slot < both[:, 1:2], both[:, 0:1] + slot, -1.0)
    places = lax.broadcasted_iota(jnp.int32, out_pick.shape, 1).astype(jnp.float32)
    out_pick[...] = jnp.where(places == row, 1.0, 0.0).astype(jnp.bfloat16)
    mine = pack[pl.ds(here, 1), :]
    from_source = mine // RPS
    is_source = jnp.where(sub == from_source, 1.0, 0.0).astype(jnp.bfloat16)
    by_k = lax.dot_general(
        lengths[...].astype(jnp.float32).astype(jnp.bfloat16), is_source, (((0,), (0,)), ((), ())),
        preferred_element_type=jnp.float32,
    )
    length = jnp.sum(jnp.where(sub == mine % RPS, by_k, 0.0), axis=0, keepdims=True)
    end = along_lanes(length)
    begin = end - length
    place = lax.broadcasted_iota(jnp.int32, (slots, RPS), 0).astype(jnp.float32)
    inside = (place >= begin) & (place < end)
    at = jnp.where(inside, from_source.astype(jnp.float32) * MAXLEN + place - begin + 1.0, 0.0)
    at = jnp.sum(at, axis=1, keepdims=True) - 1.0
    arrived = lax.broadcasted_iota(jnp.int32, in_pick.shape, 1).astype(jnp.float32)
    in_pick[...] = jnp.where(arrived == at, 1.0, 0.0).astype(jnp.bfloat16)


def make_picks(core, lengths, packing, rows):
    vm = pl.BlockSpec(memory_space=pltpu.VMEM)
    return pl.pallas_call(
        picks_kernel,
        in_specs=[pl.BlockSpec(memory_space=pltpu.SMEM), vm, vm],
        out_specs=[vm, vm],
        out_shape=[
            jax.ShapeDtypeStruct((RPS * MAXLEN, rows), jnp.bfloat16),
            jax.ShapeDtypeStruct((RPS * MAXLEN, RPS * MAXLEN), jnp.bfloat16),
        ],
        compiler_params=pltpu.CompilerParams(vmem_limit_bytes=VMEM),
        name="make_picks",
    )(core, lengths, packing.reshape(RPS, RPS))


def layer(rows, rollout, lengths, packing, norm_gain, query_weight, keyval_weight, out_weight):
    source = lax.axis_index("dp")
    tensor_index = lax.axis_index("tensor")
    core = jnp.stack([tensor_index % 2, tensor_index // 2 % 3, tensor_index // 2 % 2, source]).astype(jnp.int32)
    x = rollout[:rows]

    mine, tail = gather_rows(rollout, rows)
    gain = norm_gain.reshape(NT, 1, FS)
    wk = keyval_weight.T
    mine, tail, wk = lax.optimization_barrier((mine, tail, wk))
    theirs = swap(mine)
    keyval, inverse = project_kv(core, mine, theirs, tail, gain, wk, swap(wk))
    first = lax.ppermute(keyval, "tensor", kv_pairs(True))
    second = lax.ppermute(keyval, "tensor", kv_pairs(False))
    q, cosine, sine, bias = project_q(core, mine, theirs, tail, gain, query_weight, inverse, lengths)
    context = attend(core, q, first, second, cosine, sine, bias)
    summed, out_pick, in_pick = sum_over_chips(
        core, context, swap(context), out_weight, swap(out_weight), lengths, packing
    )
    result = (summed + x.astype(jnp.float32)).astype(jnp.bfloat16)
    outgoing = jnp.dot(out_pick, result, preferred_element_type=jnp.float32).astype(jnp.bfloat16)
    incoming = lax.all_to_all(
        outgoing.reshape(RPS, MAXLEN, FS), "dp", split_axis=0, concat_axis=0, tiled=True
    ).reshape(RPS * MAXLEN, FS)
    return jnp.dot(in_pick, incoming, preferred_element_type=jnp.float32).astype(jnp.bfloat16)


def size_kernel(lengths, size):
    longest = jnp.max(jnp.sum(lengths[...].astype(jnp.float32), axis=1, keepdims=True))
    at = jnp.int32(0)
    for cap in CAPS[:-1]:
        at += (longest > cap).astype(jnp.int32)
    size[0] = at


def body(rollout, lengths, packing, norm_gain, query_weight, keyval_weight, out_weight):
    size = pl.pallas_call(
        size_kernel,
        in_specs=[pl.BlockSpec(memory_space=pltpu.VMEM)],
        out_specs=pl.BlockSpec(memory_space=pltpu.SMEM),
        out_shape=jax.ShapeDtypeStruct((1,), jnp.int32),
        compiler_params=pltpu.CompilerParams(vmem_limit_bytes=VMEM),
        name="size",
    )(lengths)
    return lax.switch(
        size[0],
        [functools.partial(layer, cap) for cap in CAPS],
        rollout, lengths, packing, norm_gain, query_weight, keyval_weight, out_weight,
    )


def solution(mesh):
    in_specs = (
        P("dp", "tensor"),
        P(),
        P(),
        P(),
        P(None, "tensor"),
        P(None, "tensor"),
        P("tensor", None),
    )
    out_specs = P("dp", "tensor")
    return jax.shard_map(body, mesh=mesh, in_specs=in_specs, out_specs=out_specs, check_vma=False)
```

```python
import functools
import math

import jax
import jax.numpy as jnp
import numpy as np
from jax import lax
from jax.experimental import pallas as pl
from jax.experimental.pallas import tpu as pltpu
from jax.sharding import PartitionSpec as P

D = 6144
HD = 128
MAXLEN = 8
NZ = 12
NT = 24
FS = 256
RPS = 32
KVS = 64
EPS = 1e-05
ROPE_BASE = 500000.0
AG_ROWS = 168
VMEM = 12 * 1024 * 1024

Z_GROUPS = [[z * 2 + c for z in range(NZ)] for c in range(2)]
FAR = 4
NDP = 32
WIDE_GROUPS = [
    [d * NT + (3 * k + r) * 2 + c for d in range(NDP) for k in range(FAR)] for r in range(3) for c in range(2)
]
SWAP = [(t, t ^ 1) for t in range(NT)]


STEPS = 3
PER = NZ // STEPS
CAPS = (168, 176, 192, 256)


def rope_tables():
    frequency = ROPE_BASE ** (-np.arange(HD // 2) * 2.0 / HD)
    angles = np.arange(MAXLEN)[:, None] * np.concatenate([frequency, frequency])[None, :]
    sign = np.where(np.arange(HD) < HD // 2, -1.0, 1.0)[None, :]
    return np.cos(angles).astype(np.float32), (np.sin(angles) * sign).astype(np.float32)


def turn(v, cosine, sine):
    turned = jnp.concatenate([v[:, HD // 2 :], v[:, : HD // 2]], axis=1)
    return (v * cosine + turned * sine).astype(jnp.bfloat16)


def documents(lengths, source, rows):
    own = lengths[pl.ds(source, 1), :].astype(jnp.float32)
    first = lax.broadcasted_iota(jnp.int32, (RPS, RPS), 0)
    second = lax.broadcasted_iota(jnp.int32, (RPS, RPS), 1)
    column = jnp.sum(jnp.where(first == second, own, 0.0), axis=1, keepdims=True)
    end = jnp.sum(jnp.where(first <= second, column, 0.0), axis=0, keepdims=True)
    end_column = jnp.sum(jnp.where(second <= first, own, 0.0), axis=1, keepdims=True)
    start = end - own
    place = lax.broadcasted_iota(jnp.int32, (rows, RPS), 0).astype(jnp.float32)
    doc = jnp.sum(jnp.where(place >= end, 1.0, 0.0), axis=1, keepdims=True)
    begun = jnp.max(jnp.where(start <= place, start, 0.0), axis=1, keepdims=True)
    position = jnp.where(doc < RPS, place[:, :1] - begun, 0.0)
    along = lax.broadcasted_iota(jnp.int32, (RPS, rows), 1).astype(jnp.float32)
    doc_row = jnp.sum(jnp.where(along >= end_column, 1.0, 0.0), axis=0, keepdims=True)
    return doc, position, doc_row


def kv_pairs(first):
    pairs = []
    for z in range(NZ):
        g, value = z % (NZ // 2), z // (NZ // 2)
        to = 2 * g + (value if first else 1 - value)
        pairs += [(2 * z + c, 2 * to + c) for c in range(2)]
    return pairs


def swap(v):
    return lax.ppermute(v, "tensor", SWAP)


def rows_of(refs, j, side):
    head, tail = refs
    x = head[j].astype(jnp.float32)
    if tail is not None:
        x = jnp.concatenate([x, tail[2 * j + side].astype(jnp.float32)], axis=0)
    return x


def kv_kernel(has_tail, core, mine, theirs, *rest):
    if has_tail:
        tail, *rest = rest
    else:
        tail = None
    gain, wk_m, wk_t, kv_out, inv_out, kv_acc, sq_acc = rest
    step = pl.program_id(0)
    c = core[0]

    @pl.when(step == 0)
    def _():
        kv_acc[...] = jnp.zeros_like(kv_acc)
        sq_acc[...] = jnp.zeros_like(sq_acc)

    total, squares = kv_acc[...], sq_acc[...]
    for j in range(PER):
        for x_ref, side in ((mine, c), (theirs, 1 - c)):
            x = rows_of((x_ref, tail), j, side)
            square = x * x
            squares += square[:, :128] + square[:, 128:]
            scaled = (x * gain[2 * j + side]).astype(jnp.bfloat16)
            at = pl.ds(pl.multiple_of((2 * j + side) * FS, FS), FS)
            w = jnp.concatenate([wk_m[:, at], wk_t[:, at]], axis=0)
            total += lax.dot_general(
                scaled, w, (((1,), (1,)), ((), ())), preferred_element_type=jnp.float32
            )
    kv_acc[...] = total
    sq_acc[...] = squares

    @pl.when(step == STEPS - 1)
    def _():
        inverse = lax.rsqrt(jnp.sum(squares, axis=1, keepdims=True) / D + EPS)
        out = total * inverse
        turned = jnp.concatenate([out[:, KVS:], out[:, :KVS]], axis=1)
        kv_out[...] = jnp.where(c == 0, out, turned).astype(jnp.bfloat16)
        inv_out[...] = jnp.broadcast_to(inverse, inv_out.shape)


def q_kernel(has_tail, core, mine, theirs, *rest):
    if has_tail:
        tail, *rest = rest
    else:
        tail = None
    gain, wq_m, wq_t, inv, lengths, cos_t, sin_t, q_out, cos_out, sin_out, bias_out, q_acc = rest
    step = pl.program_id(0)
    c = core[0]
    rows = q_acc.shape[0]

    @pl.when(step == 0)
    def _():
        q_acc[...] = jnp.zeros_like(q_acc)
        doc, position, doc_row = documents(lengths, core[3], rows)
        cosine = jnp.broadcast_to(cos_t[0:1], (rows, HD))
        sine = jnp.broadcast_to(sin_t[0:1], (rows, HD))
        for m in range(1, MAXLEN):
            here = jnp.broadcast_to(position == m, (rows, HD))
            cosine = jnp.where(here, cos_t[m : m + 1], cosine)
            sine = jnp.where(here, sin_t[m : m + 1], sine)
        cos_out[...] = cosine
        sin_out[...] = sine
        place_q = lax.broadcasted_iota(jnp.int32, (rows, rows), 0)
        place_k = lax.broadcasted_iota(jnp.int32, (rows, rows), 1)
        allowed = (doc == doc_row) & (place_k <= place_q)
        bias_out[...] = jnp.where(allowed, 0.0, -jnp.inf)

    total = q_acc[...]
    for j in range(PER):
        for x_ref, wq, side in ((mine, wq_m, c), (theirs, wq_t, 1 - c)):
            x = rows_of((x_ref, tail), j, side)
            scaled = (x * gain[2 * j + side]).astype(jnp.bfloat16)
            total += jnp.dot(scaled, wq[j, 0], preferred_element_type=jnp.float32)
    q_acc[...] = total

    @pl.when(step == STEPS - 1)
    def _():
        for h in range(2):
            head = total[:, h * HD : (h + 1) * HD] * inv[...]
            q_out[:, h * HD : (h + 1) * HD] = turn(head, cos_out[...], sin_out[...])


def x_specs(xs, tail):
    specs = [pl.BlockSpec((PER, x.shape[1], FS), lambda i, c: (i, 0, 0)) for x in xs]
    if tail is not None:
        specs.append(pl.BlockSpec((2 * PER, tail.shape[1], FS), lambda i, c: (i, 0, 0)))
    specs.append(pl.BlockSpec((2 * PER, 1, FS), lambda i, c: (i, 0, 0)))
    return specs


def project_kv(core, mine, theirs, tail, gain, wk_m, wk_t):
    rows = mine.shape[1] + (0 if tail is None else tail.shape[1])
    whole = pl.BlockSpec((rows, HD), lambda i, c: (0, 0))
    wk_spec = pl.BlockSpec((KVS, 2 * PER * FS), lambda i, c: (0, i))
    return pl.pallas_call(
        functools.partial(kv_kernel, tail is not None),
        grid_spec=pltpu.PrefetchScalarGridSpec(
            num_scalar_prefetch=1,
            grid=(STEPS,),
            in_specs=x_specs([mine, theirs], tail) + [wk_spec, wk_spec],
            out_specs=[whole, whole],
            scratch_shapes=[pltpu.VMEM((rows, HD), jnp.float32), pltpu.VMEM((rows, HD), jnp.float32)],
        ),
        out_shape=[
            jax.ShapeDtypeStruct((rows, HD), jnp.bfloat16),
            jax.ShapeDtypeStruct((rows, HD), jnp.float32),
        ],
        compiler_params=pltpu.CompilerParams(vmem_limit_bytes=VMEM),
        cost_estimate=pl.CostEstimate(
            flops=2 * rows * D * HD, bytes_accessed=2 * D * (rows + HD), transcendentals=rows
        ),
        name="project_kv",
    )(core, mine, theirs, *([] if tail is None else [tail]), gain, wk_m, wk_t)


def project_q(core, mine, theirs, tail, gain, wq, inverse, lengths):
    rows = inverse.shape[0]
    wq4 = wq.reshape(NZ, 2, FS, FS)
    whole = lambda i, c: (0, 0)
    cos_t, sin_t = rope_tables()
    return pl.pallas_call(
        functools.partial(q_kernel, tail is not None),
        grid_spec=pltpu.PrefetchScalarGridSpec(
            num_scalar_prefetch=1,
            grid=(STEPS,),
            in_specs=x_specs([mine, theirs], tail)
            + [
                pl.BlockSpec((PER, 1, FS, FS), lambda i, c: (i, c[0], 0, 0)),
                pl.BlockSpec((PER, 1, FS, FS), lambda i, c: (i, 1 - c[0], 0, 0)),
                pl.BlockSpec((rows, HD), whole),
                pl.BlockSpec((RPS, RPS), whole),
                pl.BlockSpec((MAXLEN, HD), whole),
                pl.BlockSpec((MAXLEN, HD), whole),
            ],
            out_specs=[
                pl.BlockSpec((rows, FS), whole),
                pl.BlockSpec((rows, HD), whole),
                pl.BlockSpec((rows, HD), whole),
                pl.BlockSpec((rows, rows), whole),
            ],
            scratch_shapes=[pltpu.VMEM((rows, FS), jnp.float32)],
        ),
        out_shape=[
            jax.ShapeDtypeStruct((rows, FS), jnp.bfloat16),
            jax.ShapeDtypeStruct((rows, HD), jnp.float32),
            jax.ShapeDtypeStruct((rows, HD), jnp.float32),
            jax.ShapeDtypeStruct((rows, rows), jnp.float32),
        ],
        compiler_params=pltpu.CompilerParams(vmem_limit_bytes=VMEM),
        cost_estimate=pl.CostEstimate(
            flops=2 * rows * D * FS, bytes_accessed=2 * D * (rows + FS), transcendentals=0
        ),
        name="project_q",
    )(core, mine, theirs, *([] if tail is None else [tail]), gain, wq4, wq4, inverse,
      lengths, cos_t, sin_t)


def attention_kernel(core, q_ref, first, second, cos_ref, sin_ref, bias_ref, out_ref):
    one, two = first[...].astype(jnp.float32), second[...].astype(jnp.float32)
    swapped = core[2] == 1
    keys = jnp.where(swapped, two, one)
    values = jnp.where(swapped, one, two).astype(jnp.bfloat16)
    k_rot = turn(keys, cos_ref[...], sin_ref[...])
    for h in range(2):
        scores = lax.dot_general(
            q_ref[:, h * HD : (h + 1) * HD], k_rot, (((1,), (1,)), ((), ())), preferred_element_type=jnp.float32
        )
        masked = scores * (1 / math.sqrt(HD)) + bias_ref[...]
        exponent = jnp.exp(masked - jnp.max(masked, axis=1, keepdims=True))
        weights = (exponent / jnp.sum(exponent, axis=1, keepdims=True)).astype(jnp.bfloat16)
        context = jnp.dot(weights, values, preferred_element_type=jnp.float32)
        out_ref[:, h * HD : (h + 1) * HD] = context.astype(jnp.bfloat16)


def attend(core, q, first, second, cosine, sine, bias):
    rows = q.shape[0]
    vm = pl.BlockSpec(memory_space=pltpu.VMEM)
    return pl.pallas_call(
        attention_kernel,
        in_specs=[pl.BlockSpec(memory_space=pltpu.SMEM)] + [vm] * 6,
        out_specs=vm,
        out_shape=jax.ShapeDtypeStruct((rows, FS), jnp.bfloat16),
        compiler_params=pltpu.CompilerParams(vmem_limit_bytes=VMEM),
        cost_estimate=pl.CostEstimate(
            flops=8 * rows * rows * HD, bytes_accessed=4 * rows * FS, transcendentals=2 * rows * rows
        ),
        name="attend",
    )(core, q, first, second, cosine, sine, bias)


def out_kernel(place, mine, theirs, *rest):
    w_mine, w_theirs, outs = rest[:FAR], rest[FAR : 2 * FAR], rest[2 * FAR :]
    for at, out in enumerate(outs):

        @pl.when(pl.program_id(0) == at)
        def _():
            for k in range(FAR):
                total = jnp.dot(mine[...], w_mine[k][...], preferred_element_type=jnp.float32)
                total += jnp.dot(theirs[...], w_theirs[k][...], preferred_element_type=jnp.float32)
                out[k] = total.astype(jnp.bfloat16)


def out_project(place, mine, theirs, w_mine, w_theirs, shifts):
    rows = mine.shape[0]
    context = pl.BlockSpec((rows, FS), lambda i, p: (0, 0))
    turn_round = (lambda i, p: 1 + i + p[0] * (1 - 2 * i)) if len(shifts) == 2 else (lambda i, p: 0)
    weights = [
        pl.BlockSpec((FS, FS), lambda i, p, k=k: (0, 2 * (3 * k + lax.rem(p[1] + turn_round(i, p), 3)) + p[0]))
        for k in range(FAR)
    ]
    return pl.pallas_call(
        out_kernel,
        grid_spec=pltpu.PrefetchScalarGridSpec(
            num_scalar_prefetch=1,
            grid=(len(shifts),),
            in_specs=[context, context] + weights + weights,
            out_specs=[pl.BlockSpec((FAR, rows, FS), lambda i, p: (0, 0, 0))] * len(shifts),
        ),
        out_shape=[jax.ShapeDtypeStruct((FAR, rows, FS), jnp.bfloat16)] * len(shifts),
        compiler_params=pltpu.CompilerParams(vmem_limit_bytes=VMEM),
        cost_estimate=pl.CostEstimate(
            flops=len(shifts) * 4 * rows * FS * FAR * FS,
            bytes_accessed=len(shifts) * 2 * FAR * FS * (rows + 2 * FS),
            transcendentals=0,
        ),
        name="out_project",
    )(place, mine, theirs, *[w_mine] * FAR, *[w_theirs] * FAR)


def move_and_sum(place, x, context, theirs, w_mine, w_theirs, lengths, packing):
    one, two = out_project(place, context, theirs, w_mine, w_theirs, (1, 2))
    one, lengths, packing = lax.optimization_barrier((one, lengths, packing))
    picks = make_picks(place, lengths, packing, context.shape[0])
    below = lax.ppermute(one, "tensor", [(t, (t + 2 - 4 * (t % 2)) % NT) for t in range(NT)])
    above = lax.ppermute(two, "tensor", [(t, (t - 2 + 4 * (t % 2)) % NT) for t in range(NT)])
    (own,) = out_project(place, context, theirs, w_mine, w_theirs, (0,))
    at_home = jnp.arange(FAR)[:, None, None] == lax.axis_index("tensor") // 6
    three = own.astype(jnp.float32) + below.astype(jnp.float32) + above.astype(jnp.float32)
    three += jnp.where(at_home, x.astype(jnp.float32)[None], 0.0)
    three, out_pick, in_pick = lax.optimization_barrier((three.astype(jnp.bfloat16), *picks))
    moved = jnp.stack(
        [jnp.dot(out_pick, three[k], preferred_element_type=jnp.float32).astype(jnp.bfloat16) for k in range(FAR)]
    )
    moved = moved.reshape(FAR, RPS, MAXLEN, FS).transpose(1, 0, 2, 3).reshape(RPS * FAR, MAXLEN, FS)
    parts = lax.all_to_all(
        moved, ("dp", "tensor"), split_axis=0, concat_axis=0, tiled=True, axis_index_groups=WIDE_GROUPS
    ).reshape(RPS, FAR, MAXLEN, FS)
    incoming = jnp.sum(parts.astype(jnp.float32), axis=1).astype(jnp.bfloat16).reshape(RPS * MAXLEN, FS)
    return jnp.dot(in_pick, incoming, preferred_element_type=jnp.float32).astype(jnp.bfloat16)


def split_kernel(x_ref, head, tail):
    head[...] = x_ref[:AG_ROWS]
    last = x_ref[AG_ROWS : AG_ROWS + tail.shape[1]]
    for t in range(NT):
        tail[t] = last


def gather_rows(rollout, rows):
    if rows == AG_ROWS:
        head, tail = rollout[:rows], None
    else:
        vm = pl.BlockSpec(memory_space=pltpu.VMEM)
        head, last = pl.pallas_call(
            split_kernel,
            in_specs=[vm],
            out_specs=[vm, vm],
            out_shape=[
                jax.ShapeDtypeStruct((AG_ROWS, FS), jnp.bfloat16),
                jax.ShapeDtypeStruct((NT, rows - AG_ROWS, FS), jnp.bfloat16),
            ],
            compiler_params=pltpu.CompilerParams(vmem_limit_bytes=VMEM),
            name="split_rows",
        )(rollout)
        tail = lax.all_to_all(last, "tensor", split_axis=0, concat_axis=0, tiled=True)
    return lax.all_gather(head, "tensor", axis=0, axis_index_groups=Z_GROUPS), tail


def along_lanes(row):
    first = lax.broadcasted_iota(jnp.int32, (RPS, RPS), 0)
    second = lax.broadcasted_iota(jnp.int32, (RPS, RPS), 1)
    column = jnp.sum(jnp.where(first == second, row, 0.0), axis=1, keepdims=True)
    return jnp.sum(jnp.where(first <= second, column, 0.0), axis=0, keepdims=True)


def picks_kernel(core, lengths, pack, out_pick, in_pick):
    here = core[3]
    slots = RPS * MAXLEN
    lane = lax.broadcasted_iota(jnp.int32, (RPS, RPS), 1)
    sub = lax.broadcasted_iota(jnp.int32, (RPS, RPS), 0)
    own = lengths[pl.ds(here, 1), :].astype(jnp.float32)
    start = along_lanes(own) - own
    packed = pack[...]
    which = jnp.sum(jnp.where(packed // RPS == here, (packed % RPS).astype(jnp.float32), 0.0), axis=1, keepdims=True)
    chosen = which == lane.astype(jnp.float32)
    o_start = jnp.sum(jnp.where(chosen, start, 0.0), axis=1, keepdims=True)
    o_len = jnp.sum(jnp.where(chosen, own, 0.0), axis=1, keepdims=True)
    wide = lax.broadcasted_iota(jnp.int32, (RPS, 128), 1)
    both = jnp.where(wide == 0, o_start, jnp.where(wide == 1, o_len, 0.0)).astype(jnp.bfloat16)
    owner_of = lax.broadcasted_iota(jnp.int32, (slots, RPS), 0) // MAXLEN
    spread = jnp.where(owner_of == lax.broadcasted_iota(jnp.int32, (slots, RPS), 1), 1.0, 0.0).astype(jnp.bfloat16)
    both = jnp.dot(spread, both, preferred_element_type=jnp.float32)
    slot = (lax.broadcasted_iota(jnp.int32, (slots, 1), 0) % MAXLEN).astype(jnp.float32)
    row = jnp.where(slot < both[:, 1:2], both[:, 0:1] + slot, -1.0)
    places = lax.broadcasted_iota(jnp.int32, out_pick.shape, 1).astype(jnp.float32)
    out_pick[...] = jnp.where(places == row, 1.0, 0.0).astype(jnp.bfloat16)
    mine = pack[pl.ds(here, 1), :]
    from_source = mine // RPS
    is_source = jnp.where(sub == from_source, 1.0, 0.0).astype(jnp.bfloat16)
    by_k = lax.dot_general(
        lengths[...].astype(jnp.float32).astype(jnp.bfloat16), is_source, (((0,), (0,)), ((), ())),
        preferred_element_type=jnp.float32,
    )
    length = jnp.sum(jnp.where(sub == mine % RPS, by_k, 0.0), axis=0, keepdims=True)
    end = along_lanes(length)
    begin = end - length
    place = lax.broadcasted_iota(jnp.int32, (slots, RPS), 0).astype(jnp.float32)
    inside = (place >= begin) & (place < end)
    at = jnp.where(inside, from_source.astype(jnp.float32) * MAXLEN + place - begin + 1.0, 0.0)
    at = jnp.sum(at, axis=1, keepdims=True) - 1.0
    arrived = lax.broadcasted_iota(jnp.int32, in_pick.shape, 1).astype(jnp.float32)
    in_pick[...] = jnp.where(arrived == at, 1.0, 0.0).astype(jnp.bfloat16)


def make_picks(core, lengths, packing, rows):
    vm = pl.BlockSpec(memory_space=pltpu.VMEM)
    return pl.pallas_call(
        picks_kernel,
        in_specs=[pl.BlockSpec(memory_space=pltpu.SMEM), vm, vm],
        out_specs=[vm, vm],
        out_shape=[
            jax.ShapeDtypeStruct((RPS * MAXLEN, rows), jnp.bfloat16),
            jax.ShapeDtypeStruct((RPS * MAXLEN, RPS * MAXLEN), jnp.bfloat16),
        ],
        compiler_params=pltpu.CompilerParams(vmem_limit_bytes=VMEM),
        name="make_picks",
    )(core, lengths, packing.reshape(RPS, RPS))


def layer(rows, rollout, lengths, packing, norm_gain, query_weight, keyval_weight, out_weight):
    source = lax.axis_index("dp")
    tensor_index = lax.axis_index("tensor")
    core = jnp.stack([tensor_index % 2, tensor_index // 2 % 3, tensor_index // 2 % 2, source]).astype(jnp.int32)
    x = rollout[:rows]

    mine, tail = gather_rows(rollout, rows)
    gain = norm_gain.reshape(NT, 1, FS)
    wk = keyval_weight.T
    mine, tail, wk = lax.optimization_barrier((mine, tail, wk))
    theirs = swap(mine)
    keyval, inverse = project_kv(core, mine, theirs, tail, gain, wk, swap(wk))
    first = lax.ppermute(keyval, "tensor", kv_pairs(True))
    second = lax.ppermute(keyval, "tensor", kv_pairs(False))
    q, cosine, sine, bias = project_q(core, mine, theirs, tail, gain, query_weight, inverse, lengths)
    context = attend(core, q, first, second, cosine, sine, bias)
    return move_and_sum(
        core, x, context, swap(context), out_weight, swap(out_weight), lengths, packing
    )


def size_kernel(lengths, size):
    longest = jnp.max(jnp.sum(lengths[...].astype(jnp.float32), axis=1, keepdims=True))
    at = jnp.int32(0)
    for cap in CAPS[:-1]:
        at += (longest > cap).astype(jnp.int32)
    size[0] = at


def body(rollout, lengths, packing, norm_gain, query_weight, keyval_weight, out_weight):
    size = pl.pallas_call(
        size_kernel,
        in_specs=[pl.BlockSpec(memory_space=pltpu.VMEM)],
        out_specs=pl.BlockSpec(memory_space=pltpu.SMEM),
        out_shape=jax.ShapeDtypeStruct((1,), jnp.int32),
        compiler_params=pltpu.CompilerParams(vmem_limit_bytes=VMEM),
        name="size",
    )(lengths)
    return lax.switch(
        size[0],
        [functools.partial(layer, cap) for cap in CAPS],
        rollout, lengths, packing, norm_gain, query_weight, keyval_weight, out_weight,
    )


def solution(mesh):
    in_specs = (
        P("dp", "tensor"),
        P(),
        P(),
        P(),
        P(None, "tensor"),
        P(None, "tensor"),
        P("tensor", None),
    )
    out_specs = P("dp", "tensor")
    return jax.shard_map(body, mesh=mesh, in_specs=in_specs, out_specs=out_specs, check_vma=False)
```

```python
import functools
import math

import jax
import jax.numpy as jnp
import numpy as np
from jax import lax
from jax.experimental import pallas as pl
from jax.experimental.pallas import tpu as pltpu
from jax.sharding import PartitionSpec as P

D = 6144
HD = 128
MAXLEN = 8
NZ = 12
NT = 24
FS = 256
RPS = 32
KVS = 64
EPS = 1e-05
ROPE_BASE = 500000.0
AG_ROWS = 168
VMEM = 12 * 1024 * 1024

Z_GROUPS = [[z * 2 + c for z in range(NZ)] for c in range(2)]
FAR = 4
FAR_GROUPS = [[(3 * k + r) * 2 + c for k in range(FAR)] for r in range(3) for c in range(2)]
SWAP = [(t, t ^ 1) for t in range(NT)]


STEPS = 3
PER = NZ // STEPS
CAPS = (168, 176, 184, 192, 256)


def rope_tables():
    frequency = ROPE_BASE ** (-np.arange(HD // 2) * 2.0 / HD)
    angles = np.arange(MAXLEN)[:, None] * np.concatenate([frequency, frequency])[None, :]
    sign = np.where(np.arange(HD) < HD // 2, -1.0, 1.0)[None, :]
    return np.cos(angles).astype(np.float32), (np.sin(angles) * sign).astype(np.float32)


def turn(v, cosine, sine):
    turned = jnp.concatenate([v[:, HD // 2 :], v[:, : HD // 2]], axis=1)
    return (v * cosine + turned * sine).astype(jnp.bfloat16)


def documents(lengths, source, rows):
    own = lengths[pl.ds(source, 1), :].astype(jnp.float32)
    first = lax.broadcasted_iota(jnp.int32, (RPS, RPS), 0)
    second = lax.broadcasted_iota(jnp.int32, (RPS, RPS), 1)
    column = jnp.sum(jnp.where(first == second, own, 0.0), axis=1, keepdims=True)
    end = jnp.sum(jnp.where(first <= second, column, 0.0), axis=0, keepdims=True)
    end_column = jnp.sum(jnp.where(second <= first, own, 0.0), axis=1, keepdims=True)
    start = end - own
    place = lax.broadcasted_iota(jnp.int32, (rows, RPS), 0).astype(jnp.float32)
    doc = jnp.sum(jnp.where(place >= end, 1.0, 0.0), axis=1, keepdims=True)
    begun = jnp.max(jnp.where(start <= place, start, 0.0), axis=1, keepdims=True)
    position = jnp.where(doc < RPS, place[:, :1] - begun, 0.0)
    along = lax.broadcasted_iota(jnp.int32, (RPS, rows), 1).astype(jnp.float32)
    doc_row = jnp.sum(jnp.where(along >= end_column, 1.0, 0.0), axis=0, keepdims=True)
    return doc, position, doc_row


def kv_pairs(first):
    pairs = []
    for z in range(NZ):
        g, value = z % (NZ // 2), z // (NZ // 2)
        to = 2 * g + (value if first else 1 - value)
        pairs += [(2 * z + c, 2 * to + c) for c in range(2)]
    return pairs


def swap(v):
    return lax.ppermute(v, "tensor", SWAP)


def rows_of(refs, j, side):
    head, tail = refs
    x = head[j].astype(jnp.float32)
    if tail is not None:
        x = jnp.concatenate([x, tail[2 * j + side].astype(jnp.float32)], axis=0)
    return x


def kv_kernel(has_tail, core, mine, theirs, *rest):
    if has_tail:
        tail, *rest = rest
    else:
        tail = None
    gain, wk_m, wk_t, kv_out, inv_out, kv_acc, sq_acc = rest
    step = pl.program_id(0)
    c = core[0]

    @pl.when(step == 0)
    def _():
        kv_acc[...] = jnp.zeros_like(kv_acc)
        sq_acc[...] = jnp.zeros_like(sq_acc)

    total, squares = kv_acc[...], sq_acc[...]
    for j in range(PER):
        for x_ref, side in ((mine, c), (theirs, 1 - c)):
            x = rows_of((x_ref, tail), j, side)
            square = x * x
            squares += square[:, :128] + square[:, 128:]
            scaled = (x * gain[2 * j + side]).astype(jnp.bfloat16)
            at = pl.ds(pl.multiple_of((2 * j + side) * FS, FS), FS)
            w = jnp.concatenate([wk_m[:, at], wk_t[:, at]], axis=0)
            total += lax.dot_general(
                scaled, w, (((1,), (1,)), ((), ())), preferred_element_type=jnp.float32
            )
    kv_acc[...] = total
    sq_acc[...] = squares

    @pl.when(step == STEPS - 1)
    def _():
        inverse = lax.rsqrt(jnp.sum(squares, axis=1, keepdims=True) / D + EPS)
        out = total * inverse
        turned = jnp.concatenate([out[:, KVS:], out[:, :KVS]], axis=1)
        kv_out[...] = jnp.where(c == 0, out, turned).astype(jnp.bfloat16)
        inv_out[...] = jnp.broadcast_to(inverse, inv_out.shape)


def q_kernel(has_tail, core, mine, theirs, *rest):
    if has_tail:
        tail, *rest = rest
    else:
        tail = None
    gain, wq_m, wq_t, inv, lengths, cos_t, sin_t, q_out, cos_out, sin_out, bias_out, q_acc = rest
    step = pl.program_id(0)
    c = core[0]
    rows = q_acc.shape[0]

    @pl.when(step == 0)
    def _():
        q_acc[...] = jnp.zeros_like(q_acc)
        doc, position, doc_row = documents(lengths, core[3], rows)
        cosine = jnp.broadcast_to(cos_t[0:1], (rows, HD))
        sine = jnp.broadcast_to(sin_t[0:1], (rows, HD))
        for m in range(1, MAXLEN):
            here = jnp.broadcast_to(position == m, (rows, HD))
            cosine = jnp.where(here, cos_t[m : m + 1], cosine)
            sine = jnp.where(here, sin_t[m : m + 1], sine)
        cos_out[...] = cosine
        sin_out[...] = sine
        place_q = lax.broadcasted_iota(jnp.int32, (rows, rows), 0)
        place_k = lax.broadcasted_iota(jnp.int32, (rows, rows), 1)
        allowed = (doc == doc_row) & (place_k <= place_q)
        bias_out[...] = jnp.where(allowed, 0.0, -jnp.inf)

    total = q_acc[...]
    for j in range(PER):
        for x_ref, wq, side in ((mine, wq_m, c), (theirs, wq_t, 1 - c)):
            x = rows_of((x_ref, tail), j, side)
            scaled = (x * gain[2 * j + side]).astype(jnp.bfloat16)
            total += jnp.dot(scaled, wq[j, 0], preferred_element_type=jnp.float32)
    q_acc[...] = total

    @pl.when(step == STEPS - 1)
    def _():
        for h in range(2):
            head = total[:, h * HD : (h + 1) * HD] * inv[...]
            q_out[:, h * HD : (h + 1) * HD] = turn(head, cos_out[...], sin_out[...])


def x_specs(xs, tail):
    specs = [pl.BlockSpec((PER, x.shape[1], FS), lambda i, c: (i, 0, 0)) for x in xs]
    if tail is not None:
        specs.append(pl.BlockSpec((2 * PER, tail.shape[1], FS), lambda i, c: (i, 0, 0)))
    specs.append(pl.BlockSpec((2 * PER, 1, FS), lambda i, c: (i, 0, 0)))
    return specs


def project_kv(core, mine, theirs, tail, gain, wk_m, wk_t):
    rows = mine.shape[1] + (0 if tail is None else tail.shape[1])
    whole = pl.BlockSpec((rows, HD), lambda i, c: (0, 0))
    wk_spec = pl.BlockSpec((KVS, 2 * PER * FS), lambda i, c: (0, i))
    return pl.pallas_call(
        functools.partial(kv_kernel, tail is not None),
        grid_spec=pltpu.PrefetchScalarGridSpec(
            num_scalar_prefetch=1,
            grid=(STEPS,),
            in_specs=x_specs([mine, theirs], tail) + [wk_spec, wk_spec],
            out_specs=[whole, whole],
            scratch_shapes=[pltpu.VMEM((rows, HD), jnp.float32), pltpu.VMEM((rows, HD), jnp.float32)],
        ),
        out_shape=[
            jax.ShapeDtypeStruct((rows, HD), jnp.bfloat16),
            jax.ShapeDtypeStruct((rows, HD), jnp.float32),
        ],
        compiler_params=pltpu.CompilerParams(vmem_limit_bytes=VMEM),
        cost_estimate=pl.CostEstimate(
            flops=2 * rows * D * HD, bytes_accessed=2 * D * (rows + HD), transcendentals=rows
        ),
        name="project_kv",
    )(core, mine, theirs, *([] if tail is None else [tail]), gain, wk_m, wk_t)


def project_q(core, mine, theirs, tail, gain, wq, inverse, lengths):
    rows = inverse.shape[0]
    wq4 = wq.reshape(NZ, 2, FS, FS)
    whole = lambda i, c: (0, 0)
    cos_t, sin_t = rope_tables()
    return pl.pallas_call(
        functools.partial(q_kernel, tail is not None),
        grid_spec=pltpu.PrefetchScalarGridSpec(
            num_scalar_prefetch=1,
            grid=(STEPS,),
            in_specs=x_specs([mine, theirs], tail)
            + [
                pl.BlockSpec((PER, 1, FS, FS), lambda i, c: (i, c[0], 0, 0)),
                pl.BlockSpec((PER, 1, FS, FS), lambda i, c: (i, 1 - c[0], 0, 0)),
                pl.BlockSpec((rows, HD), whole),
                pl.BlockSpec((RPS, RPS), whole),
                pl.BlockSpec((MAXLEN, HD), whole),
                pl.BlockSpec((MAXLEN, HD), whole),
            ],
            out_specs=[
                pl.BlockSpec((rows, FS), whole),
                pl.BlockSpec((rows, HD), whole),
                pl.BlockSpec((rows, HD), whole),
                pl.BlockSpec((rows, rows), whole),
            ],
            scratch_shapes=[pltpu.VMEM((rows, FS), jnp.float32)],
        ),
        out_shape=[
            jax.ShapeDtypeStruct((rows, FS), jnp.bfloat16),
            jax.ShapeDtypeStruct((rows, HD), jnp.float32),
            jax.ShapeDtypeStruct((rows, HD), jnp.float32),
            jax.ShapeDtypeStruct((rows, rows), jnp.float32),
        ],
        compiler_params=pltpu.CompilerParams(vmem_limit_bytes=VMEM),
        cost_estimate=pl.CostEstimate(
            flops=2 * rows * D * FS, bytes_accessed=2 * D * (rows + FS), transcendentals=0
        ),
        name="project_q",
    )(core, mine, theirs, *([] if tail is None else [tail]), gain, wq4, wq4, inverse,
      lengths, cos_t, sin_t)


def attention_kernel(core, q_ref, first, second, cos_ref, sin_ref, bias_ref, out_ref):
    one, two = first[...].astype(jnp.float32), second[...].astype(jnp.float32)
    swapped = core[2] == 1
    keys = jnp.where(swapped, two, one)
    values = jnp.where(swapped, one, two).astype(jnp.bfloat16)
    k_rot = turn(keys, cos_ref[...], sin_ref[...])
    for h in range(2):
        scores = lax.dot_general(
            q_ref[:, h * HD : (h + 1) * HD], k_rot, (((1,), (1,)), ((), ())), preferred_element_type=jnp.float32
        )
        masked = scores * (1 / math.sqrt(HD)) + bias_ref[...]
        exponent = jnp.exp(masked - jnp.max(masked, axis=1, keepdims=True))
        weights = (exponent / jnp.sum(exponent, axis=1, keepdims=True)).astype(jnp.bfloat16)
        context = jnp.dot(weights, values, preferred_element_type=jnp.float32)
        out_ref[:, h * HD : (h + 1) * HD] = context.astype(jnp.bfloat16)


def attend(core, q, first, second, cosine, sine, bias):
    rows = q.shape[0]
    vm = pl.BlockSpec(memory_space=pltpu.VMEM)
    return pl.pallas_call(
        attention_kernel,
        in_specs=[pl.BlockSpec(memory_space=pltpu.SMEM)] + [vm] * 6,
        out_specs=vm,
        out_shape=jax.ShapeDtypeStruct((rows, FS), jnp.bfloat16),
        compiler_params=pltpu.CompilerParams(vmem_limit_bytes=VMEM),
        cost_estimate=pl.CostEstimate(
            flops=8 * rows * rows * HD, bytes_accessed=4 * rows * FS, transcendentals=2 * rows * rows
        ),
        name="attend",
    )(core, q, first, second, cosine, sine, bias)


def out_kernel(place, mine, theirs, *rest):
    w_mine, w_theirs, outs = rest[:FAR], rest[FAR : 2 * FAR], rest[2 * FAR :]
    for at, out in enumerate(outs):

        @pl.when(pl.program_id(0) == at)
        def _():
            for k in range(FAR):
                total = jnp.dot(mine[...], w_mine[k][...], preferred_element_type=jnp.float32)
                total += jnp.dot(theirs[...], w_theirs[k][...], preferred_element_type=jnp.float32)
                out[k] = total.astype(jnp.bfloat16)


def out_project(place, mine, theirs, w_mine, w_theirs, shifts):
    rows = mine.shape[0]
    context = pl.BlockSpec((rows, FS), lambda i, p: (0, 0))
    turn_round = (lambda i, p: 1 + i + p[0] * (1 - 2 * i)) if len(shifts) == 2 else (lambda i, p: 0)
    weights = [
        pl.BlockSpec((FS, FS), lambda i, p, k=k: (0, 2 * (3 * k + lax.rem(p[1] + turn_round(i, p), 3)) + p[0]))
        for k in range(FAR)
    ]
    return pl.pallas_call(
        out_kernel,
        grid_spec=pltpu.PrefetchScalarGridSpec(
            num_scalar_prefetch=1,
            grid=(len(shifts),),
            in_specs=[context, context] + weights + weights,
            out_specs=[pl.BlockSpec((FAR, rows, FS), lambda i, p: (0, 0, 0))] * len(shifts),
        ),
        out_shape=[jax.ShapeDtypeStruct((FAR, rows, FS), jnp.bfloat16)] * len(shifts),
        compiler_params=pltpu.CompilerParams(vmem_limit_bytes=VMEM),
        cost_estimate=pl.CostEstimate(
            flops=len(shifts) * 4 * rows * FS * FAR * FS,
            bytes_accessed=len(shifts) * 2 * FAR * FS * (rows + 2 * FS),
            transcendentals=0,
        ),
        name="out_project",
    )(place, mine, theirs, *[w_mine] * FAR, *[w_theirs] * FAR)


def sum_over_chips(place, context, theirs, w_mine, w_theirs, lengths, packing):
    one, two = out_project(place, context, theirs, w_mine, w_theirs, (1, 2))
    one, lengths, packing = lax.optimization_barrier((one, lengths, packing))
    picks = make_picks(place, lengths, packing, context.shape[0])
    below = lax.ppermute(one, "tensor", [(t, (t + 2 - 4 * (t % 2)) % NT) for t in range(NT)])
    above = lax.ppermute(two, "tensor", [(t, (t - 2 + 4 * (t % 2)) % NT) for t in range(NT)])
    (own,) = out_project(place, context, theirs, w_mine, w_theirs, (0,))
    three = own.astype(jnp.float32) + below.astype(jnp.float32) + above.astype(jnp.float32)
    three, *picks = lax.optimization_barrier((three.astype(jnp.bfloat16), *picks))
    parts = lax.all_to_all(
        three, "tensor", split_axis=0, concat_axis=0, tiled=True,
        axis_index_groups=FAR_GROUPS,
    )
    return jnp.sum(parts.astype(jnp.float32), axis=0), *picks


def split_kernel(x_ref, head, tail):
    head[...] = x_ref[:AG_ROWS]
    last = x_ref[AG_ROWS : AG_ROWS + tail.shape[1]]
    for t in range(NT):
        tail[t] = last


def gather_rows(rollout, rows):
    if rows == AG_ROWS:
        head, tail = rollout[:rows], None
    else:
        vm = pl.BlockSpec(memory_space=pltpu.VMEM)
        head, last = pl.pallas_call(
            split_kernel,
            in_specs=[vm],
            out_specs=[vm, vm],
            out_shape=[
                jax.ShapeDtypeStruct((AG_ROWS, FS), jnp.bfloat16),
                jax.ShapeDtypeStruct((NT, rows - AG_ROWS, FS), jnp.bfloat16),
            ],
            compiler_params=pltpu.CompilerParams(vmem_limit_bytes=VMEM),
            name="split_rows",
        )(rollout)
        tail = lax.all_to_all(last, "tensor", split_axis=0, concat_axis=0, tiled=True)
    return lax.all_gather(head, "tensor", axis=0, axis_index_groups=Z_GROUPS), tail


def along_lanes(row):
    first = lax.broadcasted_iota(jnp.int32, (RPS, RPS), 0)
    second = lax.broadcasted_iota(jnp.int32, (RPS, RPS), 1)
    column = jnp.sum(jnp.where(first == second, row, 0.0), axis=1, keepdims=True)
    return jnp.sum(jnp.where(first <= second, column, 0.0), axis=0, keepdims=True)


def picks_kernel(core, lengths, pack, out_pick, in_pick):
    here = core[3]
    slots = RPS * MAXLEN
    lane = lax.broadcasted_iota(jnp.int32, (RPS, RPS), 1)
    sub = lax.broadcasted_iota(jnp.int32, (RPS, RPS), 0)
    own = lengths[pl.ds(here, 1), :].astype(jnp.float32)
    start = along_lanes(own) - own
    packed = pack[...]
    which = jnp.sum(jnp.where(packed // RPS == here, (packed % RPS).astype(jnp.float32), 0.0), axis=1, keepdims=True)
    chosen = which == lane.astype(jnp.float32)
    o_start = jnp.sum(jnp.where(chosen, start, 0.0), axis=1, keepdims=True)
    o_len = jnp.sum(jnp.where(chosen, own, 0.0), axis=1, keepdims=True)
    wide = lax.broadcasted_iota(jnp.int32, (RPS, 128), 1)
    both = jnp.where(wide == 0, o_start, jnp.where(wide == 1, o_len, 0.0)).astype(jnp.bfloat16)
    owner_of = lax.broadcasted_iota(jnp.int32, (slots, RPS), 0) // MAXLEN
    spread = jnp.where(owner_of == lax.broadcasted_iota(jnp.int32, (slots, RPS), 1), 1.0, 0.0).astype(jnp.bfloat16)
    both = jnp.dot(spread, both, preferred_element_type=jnp.float32)
    slot = (lax.broadcasted_iota(jnp.int32, (slots, 1), 0) % MAXLEN).astype(jnp.float32)
    row = jnp.where(slot < both[:, 1:2], both[:, 0:1] + slot, -1.0)
    places = lax.broadcasted_iota(jnp.int32, out_pick.shape, 1).astype(jnp.float32)
    out_pick[...] = jnp.where(places == row, 1.0, 0.0).astype(jnp.bfloat16)
    mine = pack[pl.ds(here, 1), :]
    from_source = mine // RPS
    is_source = jnp.where(sub == from_source, 1.0, 0.0).astype(jnp.bfloat16)
    by_k = lax.dot_general(
        lengths[...].astype(jnp.float32).astype(jnp.bfloat16), is_source, (((0,), (0,)), ((), ())),
        preferred_element_type=jnp.float32,
    )
    length = jnp.sum(jnp.where(sub == mine % RPS, by_k, 0.0), axis=0, keepdims=True)
    end = along_lanes(length)
    begin = end - length
    place = lax.broadcasted_iota(jnp.int32, (slots, RPS), 0).astype(jnp.float32)
    inside = (place >= begin) & (place < end)
    at = jnp.where(inside, from_source.astype(jnp.float32) * MAXLEN + place - begin + 1.0, 0.0)
    at = jnp.sum(at, axis=1, keepdims=True) - 1.0
    arrived = lax.broadcasted_iota(jnp.int32, in_pick.shape, 1).astype(jnp.float32)
    in_pick[...] = jnp.where(arrived == at, 1.0, 0.0).astype(jnp.bfloat16)


def make_picks(core, lengths, packing, rows):
    vm = pl.BlockSpec(memory_space=pltpu.VMEM)
    return pl.pallas_call(
        picks_kernel,
        in_specs=[pl.BlockSpec(memory_space=pltpu.SMEM), vm, vm],
        out_specs=[vm, vm],
        out_shape=[
            jax.ShapeDtypeStruct((RPS * MAXLEN, rows), jnp.bfloat16),
            jax.ShapeDtypeStruct((RPS * MAXLEN, RPS * MAXLEN), jnp.bfloat16),
        ],
        compiler_params=pltpu.CompilerParams(vmem_limit_bytes=VMEM),
        name="make_picks",
    )(core, lengths, packing.reshape(RPS, RPS))


def layer(rows, rollout, lengths, packing, norm_gain, query_weight, keyval_weight, out_weight):
    source = lax.axis_index("dp")
    tensor_index = lax.axis_index("tensor")
    core = jnp.stack([tensor_index % 2, tensor_index // 2 % 3, tensor_index // 2 % 2, source]).astype(jnp.int32)
    x = rollout[:rows]

    mine, tail = gather_rows(rollout, rows)
    gain = norm_gain.reshape(NT, 1, FS)
    wk = keyval_weight.T
    mine, tail, wk = lax.optimization_barrier((mine, tail, wk))
    theirs = swap(mine)
    keyval, inverse = project_kv(core, mine, theirs, tail, gain, wk, swap(wk))
    first = lax.ppermute(keyval, "tensor", kv_pairs(True))
    second = lax.ppermute(keyval, "tensor", kv_pairs(False))
    q, cosine, sine, bias = project_q(core, mine, theirs, tail, gain, query_weight, inverse, lengths)
    context = attend(core, q, first, second, cosine, sine, bias)
    summed, out_pick, in_pick = sum_over_chips(
        core, context, swap(context), out_weight, swap(out_weight), lengths, packing
    )
    result = (summed + x.astype(jnp.float32)).astype(jnp.bfloat16)
    outgoing = jnp.dot(out_pick, result, preferred_element_type=jnp.float32).astype(jnp.bfloat16)
    incoming = lax.all_to_all(
        outgoing.reshape(RPS, MAXLEN, FS), "dp", split_axis=0, concat_axis=0, tiled=True
    ).reshape(RPS * MAXLEN, FS)
    return in_pick, incoming


def size_kernel(lengths, size):
    longest = jnp.max(jnp.sum(lengths[...].astype(jnp.float32), axis=1, keepdims=True))
    at = jnp.int32(0)
    for cap in CAPS[:-1]:
        at += (longest > cap).astype(jnp.int32)
    size[0] = at


def body(rollout, lengths, packing, norm_gain, query_weight, keyval_weight, out_weight):
    size = pl.pallas_call(
        size_kernel,
        in_specs=[pl.BlockSpec(memory_space=pltpu.VMEM)],
        out_specs=pl.BlockSpec(memory_space=pltpu.SMEM),
        out_shape=jax.ShapeDtypeStruct((1,), jnp.int32),
        compiler_params=pltpu.CompilerParams(vmem_limit_bytes=VMEM),
        name="size",
    )(lengths)
    in_pick, incoming = lax.switch(
        size[0],
        [functools.partial(layer, cap) for cap in CAPS],
        rollout, lengths, packing, norm_gain, query_weight, keyval_weight, out_weight,
    )
    return jnp.dot(in_pick, incoming, preferred_element_type=jnp.float32).astype(jnp.bfloat16)


def solution(mesh):
    in_specs = (
        P("dp", "tensor"),
        P(),
        P(),
        P(),
        P(None, "tensor"),
        P(None, "tensor"),
        P("tensor", None),
    )
    out_specs = P("dp", "tensor")
    return jax.shard_map(body, mesh=mesh, in_specs=in_specs, out_specs=out_specs, check_vma=False)
```
